32 devices in a mesh: dp: 4 (over y, x), graph: 8 (over z, core).
Axes of the slice: x: 2, y: 2, z: 4, core: 2. Of those that a mesh axis runs over, the one named last changes fastest.
Arguments:
- node_feats: bfloat16 [4, 256, 49, 128], P('dp', 'graph'), may hold values from -6 to 6
- cotangent: bfloat16 [4, 256, 49, 128], P('dp', 'graph'), may hold values from -10 to 10
- sources: int32 [4, 2048], P('dp', 'graph'), may hold values from 0 to 255, as said below
- targets: int32 [4, 2048], P('dp', 'graph'), may hold values from 0 to 255, as said below
- bins: int32 [4, 2048], P('dp', 'graph'), may hold values from 0 to 63
- live_mask: int32 [4, 2048], P('dp', 'graph'), may hold values from 0 to 1, as said below
- radial: bfloat16 [4, 2048, 512], P('dp', 'graph'), may hold values from 0 to 1
- edge_bias: bfloat16 [4, 2048, 8], P('dp', 'graph'), may hold values from -4 to 256
- w_value: bfloat16 [128, 128], replicated, may hold values from -0.5 to 0.5
- w_query: bfloat16 [128, 128], replicated, may hold values from -0.5 to 0.5
- w_out: bfloat16 [128, 128], replicated, may hold values from -0.5 to 0.5
- w_radial: bfloat16 [512, 128], replicated, may hold values from -0.25 to 0.25
- w_mix: bfloat16 [5, 128, 128], replicated, may hold values from -0.5 to 0.5
- rotations: bfloat16 [64, 49, 49], replicated, may hold values from -1 to 3, as said below
Outputs:
- updated: bfloat16 [4, 256, 49, 128], P('dp', 'graph')
- grad_nodes: bfloat16 [4, 256, 49, 128], P('dp', 'graph')
- grad_value: float32 [128, 128], replicated
- grad_query: float32 [128, 128], replicated
- grad_out: float32 [128, 128], replicated
- grad_radial: float32 [512, 128], replicated
- grad_mix: float32 [5, 128, 128], replicated
The draws below stay inside these ranges and needn't reach their ends.
Inputs may be any that keep to these rules, and one draw needn't show every extreme that they name: `sources`: every slot of graph index j's block of 256 slots names a source node owned by j, one of nodes j * 32 to j * 32 + 31. `targets`: in each device's block of 256 slots, slots j * 32 to j * 32 + 31 hold edges into nodes j * 32 to j * 32 + 31, owned by graph index j. `live_mask`: in each group of 32 slots the live slots come first; in every batch some owner receives 32 live edges from every device's block. `rotations`: entry (i, j) of a rotation is zero unless i and j lie in the same degree block l*l to l*l + 2l.
All inputs are finite; a program needn't handle non-finite values.
Results may differ from the reference program's by a relative error of at most 0.012.
Values may be sent and summed in bfloat16 or wider, within the bound.
No kernel may reach another device: no remote copies, remote signals or barrier semaphores. Data moves between devices by JAX's collectives and lax.ppermute only.
A program may use at most 128 MiB of HBM per device.

```python
import math
import jax
import jax.numpy as jnp
import numpy as np
from jax import lax

C = 128
H = 8
VH = 16
NR = 512
LMAX = 6
MMAX = 2
BINS = 64
N_DEV = 32
E_DEV = 256
VC = 128
K = 49
CAP = 32
NODES = 256
EDGES = 2048
BATCHES = 4


def edge_layout(key):
    base_key = jax.random.fold_in(key, 7)
    count_key, hot_key, pick_key = jax.random.split(base_key, 3)
    groups = E_DEV // CAP
    counts = jax.random.randint(count_key, (BATCHES, groups, groups), 0, CAP + 1)
    hottest = jax.random.randint(hot_key, (BATCHES, 1, 1), 0, groups)
    owner_ids = jnp.arange(groups, dtype=jnp.int32)
    counts = jnp.where(owner_ids[None, None, :] == hottest, CAP, counts)
    slot_ids = jnp.arange(CAP, dtype=jnp.int32)
    live_slots = (slot_ids[None, None, None, :] < counts[..., None]).astype(jnp.int32)
    local_ids = jax.random.randint(pick_key, (BATCHES, groups, groups, CAP), 0, N_DEV)
    target_ids = owner_ids[None, None, :, None] * N_DEV + local_ids
    return (target_ids.reshape(BATCHES, groups * E_DEV), live_slots.reshape(BATCHES, groups * E_DEV))


def draw_targets(key, part):
    return edge_layout(key)[0].astype(jnp.int32)


def draw_live_mask(key, part):
    return edge_layout(key)[1].astype(jnp.int32)


def draw_sources(key, part):
    key = jax.random.fold_in(key, 31)
    groups = E_DEV // CAP
    local_ids = jax.random.randint(key, (BATCHES, groups, E_DEV), 0, N_DEV)
    owner_base = jnp.arange(groups, dtype=jnp.int32)[None, :, None] * N_DEV
    return (owner_base + local_ids).reshape(BATCHES, groups * E_DEV).astype(jnp.int32)


def draw_cotangent(key, part):
    entry_key = jax.random.fold_in(key, 23)
    steps = jnp.arange(BATCHES, dtype=jnp.float32) / max(BATCHES - 1, 1)
    batch_scale = 0.4 * jnp.exp(steps * math.log(6.25))
    entries = jnp.clip(jax.random.normal(entry_key, (BATCHES, NODES, K, C), jnp.float32), -4.0, 4.0)
    return (entries * batch_scale[:, None, None, None]).astype(jnp.bfloat16)


def draw_edge_bias(key, part):
    noise_key = jax.random.fold_in(jax.random.fold_in(key, 13), 0)
    noise = jnp.clip(jax.random.normal(noise_key, (BATCHES, EDGES, H), jnp.float32), -4.0, 4.0)
    return noise.astype(jnp.bfloat16)


def draw_rotations(key, part):
    degree_of = np.repeat(np.arange(LMAX + 1), 2 * np.arange(LMAX + 1) + 1)
    same_block = jnp.asarray(degree_of[:, None] == degree_of[None, :])
    widths = jnp.asarray(np.sqrt(2.0 * degree_of + 1.0), jnp.float32)[:, None]
    entry_key = jax.random.fold_in(key, 17)
    entries = jnp.clip(jax.random.normal(entry_key, (BINS, K, K), jnp.float32), -4.0, 4.0)
    table = jnp.where(same_block[None], jnp.eye(K, dtype=jnp.float32)[None] + 0.5 * entries / widths[None], 0.0)
    return table.astype(jnp.bfloat16)


def with_ends(values, rng, least, top_value):
    place = [jax.random.randint(jax.random.fold_in(rng, axis), (), 0, length) for axis, length in enumerate(values.shape)]
    longest = values.shape.index(max(values.shape))
    beside = place[:longest] + [(place[longest] + 1) % values.shape[longest]] + place[longest + 1:]
    return values.at[tuple(place)].set(least).at[tuple(beside)].set(top_value)


def shard_levels(rng, extent, cuts, low, largest):
    factor_of = 1.0
    for dim, blocks in cuts:
        heights = jax.random.uniform(jax.random.fold_in(jax.random.fold_in(rng, 6), dim), (blocks,), jnp.float32, low / len(cuts), largest / len(cuts))
        factor_of = factor_of * jnp.repeat(jnp.exp(heights), extent[dim] // blocks).reshape((-1,) + (1,) * (len(extent) - 1 - dim))
    return factor_of


def scatter_about(own_key, shape, width, bound, cuts=(), kind=jnp.bfloat16):
    gain = shard_levels(own_key, shape, cuts, -0.22, 0.18) if cuts else 1.0
    values = jax.random.normal(own_key, shape, jnp.float32) * width * gain
    return jnp.minimum(jnp.maximum(values, -bound), bound).astype(kind)


def setup_inputs(seed: int = 0) -> dict:
    arg_keys = jax.random.split(jax.random.key(seed), 15)
    node_feats = scatter_about(arg_keys[0], (BATCHES, NODES, K, C), 1.0, 6.0, ((0, 4), (1, 8)))
    cotangent = draw_cotangent(jax.random.fold_in(arg_keys[14], 71), 0)
    sources = draw_sources(jax.random.fold_in(arg_keys[14], 71), 0)
    targets = draw_targets(jax.random.fold_in(arg_keys[14], 71), 0)
    bins = with_ends(jax.random.randint(arg_keys[4], (BATCHES, EDGES), 0, BINS), jax.random.fold_in(arg_keys[4], 1), 0, BINS - 1).astype(jnp.int32)
    live_mask = draw_live_mask(jax.random.fold_in(arg_keys[14], 71), 0)
    radial = jnp.clip(1.0 * jax.random.uniform(arg_keys[6], (BATCHES, EDGES, NR), jnp.float32) ** shard_levels(arg_keys[6], (BATCHES, EDGES, NR), ((0, 4), (1, 8)), -0.2, 0.2), 0.0, 1.0).astype(jnp.bfloat16)
    edge_bias = draw_edge_bias(jax.random.fold_in(arg_keys[14], 71), 0)
    w_value = scatter_about(arg_keys[8], (C, VC), C ** -0.5, 0.5)
    w_query = scatter_about(arg_keys[9], (C, VC), C ** -0.5, 0.5)
    w_out = scatter_about(arg_keys[10], (VC, C), VC ** -0.5, 0.5)
    w_radial = scatter_about(arg_keys[11], (NR, VC), NR ** -0.5, 0.25)
    w_mix = scatter_about(arg_keys[12], (2 * MMAX + 1, VC, VC), VC ** -0.5, 0.5)
    rotations = draw_rotations(jax.random.fold_in(arg_keys[14], 71), 0)
    return dict(node_feats=node_feats, cotangent=cotangent, sources=sources, targets=targets, bins=bins, live_mask=live_mask, radial=radial, edge_bias=edge_bias, w_value=w_value, w_query=w_query, w_out=w_out, w_radial=w_radial, w_mix=w_mix, rotations=rotations)


def frame_rows():
    row_list = [degree * degree + degree for degree in range(LMAX + 1)]
    for order in range(1, MMAX + 1):
        row_list += [degree * degree + degree + order for degree in range(order, LMAX + 1)]
        row_list += [degree * degree + degree - order for degree in range(order, LMAX + 1)]
    return np.array(row_list, dtype=np.int32)

def project(left, right):
    return jnp.einsum('erc,cd->erd', left.astype(jnp.float32), right.astype(jnp.float32))

def project_back(left, right):
    return jnp.einsum('erd,cd->erc', left.astype(jnp.float32), right.astype(jnp.float32))

def outer_sum(left, right):
    return jnp.einsum('erc,erd->cd', left.astype(jnp.float32), right.astype(jnp.float32))

def head_sum(inputs):
    return lax.optimization_barrier(jnp.sum(inputs.reshape(inputs.shape[:-1] + (H, VH)), axis=-1))

def mix_forward(scaled, w_mix):
    pieces = [project(scaled[:, :LMAX + 1], w_mix[0])]
    offset = LMAX + 1
    for order in range(1, MMAX + 1):
        length = LMAX + 1 - order
        plus_rows = scaled[:, offset:offset + length]
        minus_rows = scaled[:, offset + length:offset + 2 * length]
        pieces.append(project(plus_rows, w_mix[2 * order - 1]) - project(minus_rows, w_mix[2 * order]))
        pieces.append(project(minus_rows, w_mix[2 * order - 1]) + project(plus_rows, w_mix[2 * order]))
        offset += 2 * length
    return jnp.concatenate(pieces, axis=1)

def mix_backward(scaled, dmixed, w_mix):
    pieces = [project_back(dmixed[:, :LMAX + 1], w_mix[0])]
    grad_list = [outer_sum(scaled[:, :LMAX + 1], dmixed[:, :LMAX + 1])]
    offset = LMAX + 1
    for order in range(1, MMAX + 1):
        length = LMAX + 1 - order
        plus_rows = scaled[:, offset:offset + length]
        minus_rows = scaled[:, offset + length:offset + 2 * length]
        plus_grad = dmixed[:, offset:offset + length]
        minus_grad = dmixed[:, offset + length:offset + 2 * length]
        weight_even = w_mix[2 * order - 1]
        weight_odd = w_mix[2 * order]
        pieces.append(project_back(plus_grad, weight_even) + project_back(minus_grad, weight_odd))
        pieces.append(project_back(minus_grad, weight_even) - project_back(plus_grad, weight_odd))
        grad_list.append(outer_sum(plus_rows, plus_grad) + outer_sum(minus_rows, minus_grad))
        grad_list.append(outer_sum(plus_rows, minus_grad) - outer_sum(minus_rows, plus_grad))
        offset += 2 * length
    return (jnp.concatenate(pieces, axis=1), jnp.stack(grad_list))

def batch_pass(inputs, w_value, w_query, w_out, w_radial, w_mix, rotations):
    features, cot_rows, source_ids, target_ids, bin_ids, live_ids, radial, bias_rows = inputs
    values = jnp.einsum('nkc,cd->nkd', features.astype(jnp.float32), w_value.astype(jnp.float32)).astype(jnp.bfloat16)
    queries = jnp.dot(features[:, 0, :], w_query, preferred_element_type=jnp.float32).astype(jnp.bfloat16)
    turning = rotations[:, frame_rows(), :][bin_ids].astype(jnp.float32)
    incoming = values[source_ids].astype(jnp.float32)
    framed = jnp.einsum('erk,ekc->erc', turning, incoming)
    gating = jax.nn.sigmoid(jnp.dot(radial, w_radial, preferred_element_type=jnp.float32))
    scaled = (framed * gating[:, None, :]).astype(jnp.bfloat16)
    mixed_rows = mix_forward(scaled, w_mix).astype(jnp.bfloat16)
    rotated = jnp.einsum('erk,erc->ekc', turning, mixed_rows.astype(jnp.float32))
    query_rows = queries[target_ids]
    scores = head_sum(mixed_rows[:, 0, :].astype(jnp.float32) * query_rows.astype(jnp.float32)) / math.sqrt(VH) + bias_rows.astype(jnp.float32)
    live_col = (live_ids == 1)[:, None]
    seg_top = jax.ops.segment_max(jnp.where(live_col, scores, 0.0), target_ids, num_segments=NODES)
    top_score = jnp.maximum(seg_top, 0.0)
    weight = jnp.where(live_col, jnp.exp(jnp.where(live_col, scores - top_score[target_ids], 0.0)), 0.0)
    denominator = jnp.exp(-top_score) + jax.ops.segment_sum(weight, target_ids, num_segments=NODES)
    spread = jnp.repeat(weight, VH, axis=1)
    collected = jax.ops.segment_sum(rotated * spread[:, None, :], target_ids, num_segments=NODES)
    attended = collected / jnp.repeat(denominator, VH, axis=1)[:, None, :]
    attended_b = attended.astype(jnp.bfloat16)
    updated = (features.astype(jnp.float32) + jnp.einsum('nkd,dc->nkc', attended_b.astype(jnp.float32), w_out.astype(jnp.float32))).astype(jnp.bfloat16)
    dattended = jnp.einsum('nkc,dc->nkd', cot_rows.astype(jnp.float32), w_out.astype(jnp.float32)).astype(jnp.bfloat16)
    grad_out = jnp.einsum('nkd,nkc->dc', attended_b.astype(jnp.float32), cot_rows.astype(jnp.float32))
    dot_head = head_sum(lax.optimization_barrier(jnp.sum(dattended.astype(jnp.float32) * attended, axis=1)))
    attention_share = weight / denominator[target_ids]
    dattended_rows = dattended[target_ids].astype(jnp.float32)
    dalpha = head_sum(lax.optimization_barrier(jnp.sum(dattended_rows * rotated, axis=1)))
    dscore = attention_share * (dalpha - dot_head[target_ids])
    dback_rows = (dattended_rows * jnp.repeat(attention_share, VH, axis=1)[:, None, :]).astype(jnp.bfloat16)
    dlogit = jnp.repeat(dscore, VH, axis=1) / math.sqrt(VH)
    dmixed = jnp.einsum('erk,ekc->erc', turning, dback_rows.astype(jnp.float32))
    dmixed = dmixed.at[:, 0, :].add(dlogit * query_rows.astype(jnp.float32)).astype(jnp.bfloat16)
    dscaled, grad_mix = mix_backward(scaled, dmixed, w_mix)
    dframed = (dscaled * gating[:, None, :]).astype(jnp.bfloat16)
    dgating = lax.optimization_barrier(jnp.sum(dscaled * framed, axis=1))
    dgate_in = (dgating * gating * (1.0 - gating)).astype(jnp.bfloat16)
    grad_radial = jnp.einsum('ef,ec->fc', radial.astype(jnp.float32), dgate_in.astype(jnp.float32))
    dsource = jnp.einsum('erk,erc->ekc', turning, dframed.astype(jnp.float32))
    dvalue = jnp.zeros((NODES, K, VC), jnp.float32).at[source_ids].add(dsource)
    dquery = jax.ops.segment_sum(dlogit * mixed_rows[:, 0, :].astype(jnp.float32), target_ids, num_segments=NODES)
    dvalue_b = dvalue.astype(jnp.bfloat16)
    dquery_b = dquery.astype(jnp.bfloat16)
    grad_value = jnp.einsum('nkc,nkd->cd', features.astype(jnp.float32), dvalue_b.astype(jnp.float32))
    grad_query = jnp.einsum('nc,nd->cd', features[:, 0, :].astype(jnp.float32), dquery_b.astype(jnp.float32))
    grad_nodes = cot_rows.astype(jnp.float32) + jnp.einsum('nkd,cd->nkc', dvalue_b.astype(jnp.float32), w_value.astype(jnp.float32))
    grad_nodes = grad_nodes.at[:, 0, :].add(jnp.einsum('nd,cd->nc', dquery_b.astype(jnp.float32), w_query.astype(jnp.float32)))
    return (updated, grad_nodes.astype(jnp.bfloat16), grad_value, grad_query, grad_out, grad_radial, grad_mix)

def reference(node_feats, cotangent, sources, targets, bins, live_mask, radial, edge_bias, w_value, w_query, w_out, w_radial, w_mix, rotations):

    def per_batch(inputs):
        return batch_pass(inputs, w_value, w_query, w_out, w_radial, w_mix, rotations)
    results = lax.map(per_batch, (node_feats, cotangent, sources, targets, bins, live_mask, radial, edge_bias))
    updated, grad_nodes, grad_value, grad_query, grad_out, grad_radial, grad_mix = results
    return (updated, grad_nodes, lax.optimization_barrier(jnp.sum(grad_value, axis=0)), lax.optimization_barrier(jnp.sum(grad_query, axis=0)), lax.optimization_barrier(jnp.sum(grad_out, axis=0)), lax.optimization_barrier(jnp.sum(grad_radial, axis=0)), lax.optimization_barrier(jnp.sum(grad_mix, axis=0)))
```

```python
import functools

import jax
import jax.numpy as jnp
import numpy as np
from jax import lax
from jax.experimental import pallas as pl
from jax.experimental.pallas import tpu as pltpu
from jax.sharding import PartitionSpec as P

H = 8
VH = 16
LMAX = 6
MMAX = 2
K = (LMAX + 1) ** 2
BF = jnp.bfloat16
F32 = jnp.float32
CHUNK = 16
LANES = 128


def frame_layout():
    index, degree_of = [], []
    for order in range(MMAX + 1):
        for sign in (1, -1) if order else (1,):
            for degree in range(order, LMAX + 1):
                index.append(degree * degree + degree + sign * order)
                degree_of.append(degree)
    return index, degree_of


ROWS, DEGREE = frame_layout()
R = len(ROWS)
OF_DEGREE = [[r for r in range(R) if DEGREE[r] == degree] for degree in range(LMAX + 1)]
PAIRS = []
_offset = LMAX + 1
for _order in range(1, MMAX + 1):
    _length = LMAX + 1 - _order
    for _i in range(_length):
        PAIRS.append((_order, _offset + _i, _offset + _length + _i))
    _offset += 2 * _length


def dot(a, b, ca=1, cb=0, exact=False):
    return lax.dot_general(
        a,
        b,
        (((ca,), (cb,)), ((), ())),
        precision=lax.Precision.HIGHEST if exact else None,
        preferred_element_type=F32,
    )


def flip(a):
    return jnp.transpose(a.astype(F32)).astype(a.dtype)


def hits(row, count, dtype):
    lines = lax.broadcasted_iota(jnp.int32, (count, row.shape[1]), 0)
    return jnp.where(lines == row.astype(jnp.int32), 1.0, 0.0).astype(dtype)


def head_sum(a):
    return jnp.sum(a.reshape(H, VH, a.shape[1]), axis=1)


def spread(a):
    return jnp.broadcast_to(a[:, None, :], (H, VH, a.shape[1])).reshape(H * VH, a.shape[1])


def turn(table, source, degrees, emit):
    channels, edges = source.shape[1], source.shape[2]

    def step(i, carry):
        rows = pl.ds(pl.multiple_of(i * CHUNK, CHUNK), CHUNK)
        for start in range(0, edges, LANES):
            lanes = pl.ds(start, LANES)
            for degree in degrees:
                block = range(degree * degree, (degree + 1) ** 2)
                parts = [source[k, rows, lanes].astype(F32) for k in block]
                for r in OF_DEGREE[degree]:
                    total = None
                    for k, part in zip(block, parts):
                        term = table[r, k : k + 1, start : start + LANES] * part
                        total = term if total is None else total + term
                    emit(r, rows, lanes, total)
        return carry

    lax.fori_loop(0, channels // CHUNK, step, 0)


def turn_back(table, source, degrees, out):
    channels, edges = source.shape[1], source.shape[2]

    def step(i, carry):
        rows = pl.ds(pl.multiple_of(i * CHUNK, CHUNK), CHUNK)
        for start in range(0, edges, LANES):
            lanes = pl.ds(start, LANES)
            for degree in degrees:
                parts = [source[r, rows, lanes].astype(F32) for r in OF_DEGREE[degree]]
                for k in range(degree * degree, (degree + 1) ** 2):
                    total = None
                    for r, part in zip(OF_DEGREE[degree], parts):
                        term = table[r, k : k + 1, start : start + LANES] * part
                        total = term if total is None else total + term
                    out[k, rows, lanes] = total.astype(out.dtype)
        return carry

    lax.fori_loop(0, channels // CHUNK, step, 0)


def each_k(body, first=0):
    def step(i, carry):
        for j in range(LMAX + 1):
            body(i * (LMAX + 1) + j)
        return carry

    lax.fori_loop(0, LMAX + 1, step, 0)


def mix_block(w_mix, order, back):
    even, odd = w_mix[2 * order - 1], w_mix[2 * order]
    if back:
        return jnp.concatenate(
            [
                jnp.concatenate([even, odd], axis=1),
                jnp.concatenate([-odd, even], axis=1),
            ],
            axis=0,
        )
    even, odd = flip(even), flip(odd)
    return jnp.concatenate(
        [
            jnp.concatenate([even, -odd], axis=1),
            jnp.concatenate([odd, even], axis=1),
        ],
        axis=0,
    )


def forward_kernel(chips, core, *refs):
    (pack_own, pack_sib, radial_own, radial_sib, feats_own, feats_sib) = refs[:6]
    firsts = refs[6 : 6 + chips]
    (w_value, w_query, w_radial, w_mix, rot) = refs[6 + chips : 11 + chips]
    (table, scaled, mixed, gating, pack, radial, weight, stats, query) = refs[11 + chips : 20 + chips]
    (incoming,) = refs[20 + chips :]
    slots = pack_own.shape[1]
    cap = slots // (2 * chips)
    half = slots // 2
    nodes = feats_own.shape[1]
    targets = chips * nodes
    bins = rot.shape[2]

    edge = lax.broadcasted_iota(jnp.int32, (2 * slots, slots), 1)
    place = lax.broadcasted_iota(jnp.int32, (2 * slots, slots), 0)
    within = edge % half
    origin = (edge // half) * slots + (2 * (within // cap) + core[0]) * cap + within % cap
    pick = jnp.where(place == origin, 1.0, 0.0).astype(BF)
    packs = jnp.concatenate([pack_own[...], pack_sib[...]], axis=1).astype(BF)
    rows = dot(packs, pick)
    pack[...] = rows
    radial[...] = dot(
        pick, jnp.concatenate([radial_own[...], radial_sib[...]], axis=0), 0, 0
    ).astype(BF)
    gating[...] = jax.nn.sigmoid(dot(flip(w_radial[...]), radial[...], 1, 1))

    bin_hit = hits(rows[2:3], bins, BF)
    for r, row in enumerate(ROWS):
        table[r, 0:K, :] = dot(rot[row], bin_hit)
    source_hit = hits(rows[0:1], 2 * nodes, BF)
    value_t = flip(w_value[...])

    def gather(k):
        here = jnp.concatenate([feats_own[k], feats_sib[k]], axis=0)
        values = dot(value_t, here, 1, 1).astype(BF)
        incoming[k] = dot(values, source_hit).astype(BF)

    each_k(gather)

    def emit(r, rows_, lanes, total):
        scaled[r, rows_, lanes] = (total * gating[rows_, lanes]).astype(BF)

    turn(table, incoming, range(LMAX + 1), emit)

    zero_t = flip(w_mix[0])
    for r in range(LMAX + 1):
        mixed[r] = dot(zero_t, scaled[r]).astype(BF)
    blocks = [None] + [mix_block(w_mix, order, False) for order in range(1, MMAX + 1)]
    for order, plus, minus in PAIRS:
        both = jnp.concatenate([scaled[plus], scaled[minus]], axis=0)
        out = dot(blocks[order], both).astype(BF)
        mixed[plus] = out[: H * VH]
        mixed[minus] = out[H * VH :]

    target_hit = hits(rows[1:2], targets, BF)
    first = jnp.concatenate([f[...] for f in firsts], axis=0)
    queries = dot(flip(w_query[...]), first, 1, 1).astype(BF)
    query[...] = dot(queries, target_hit)
    scores = head_sum(mixed[0].astype(F32) * query[...]) * (1.0 / VH**0.5) + rows[8:16]
    live = rows[3:4] > 0.5
    columns = jnp.transpose(rows)
    score_columns = jnp.transpose(scores)
    line = lax.broadcasted_iota(jnp.int32, (slots, targets), 1)
    chosen = (line == columns[:, 1:2].astype(jnp.int32)) & (columns[:, 3:4] > 0.5)
    top = jnp.concatenate(
        [
            jnp.max(jnp.where(chosen, score_columns[:, h : h + 1], 0.0), axis=0, keepdims=True)
            for h in range(H)
        ],
        axis=0,
    )
    top = jnp.maximum(top, 0.0)
    target_hit32 = target_hit.astype(F32)
    top_edge = dot(top, target_hit32, exact=True)
    weights = jnp.where(live, jnp.exp(jnp.where(live, scores - top_edge, 0.0)), 0.0)
    weight[...] = weights
    stats[0:H] = top
    stats[H : 2 * H] = dot(weights, target_hit32, 1, 1, exact=True)


def attend_kernel(chips, *refs):
    stats = refs[:chips]
    weight, pack, table, mixed = refs[chips : chips + 4]
    share = refs[chips + 4]
    parts = refs[chips + 5 : 2 * chips + 5]
    scaled_rows, back = refs[2 * chips + 5 :]
    targets = stats[0].shape[1]
    nodes = targets // chips
    target_hit = hits(pack[1:2], targets, BF)
    tops, sums = [], []
    for p in range(chips):
        pieces = [stats[p][:, (q ^ p) * nodes : ((q ^ p) + 1) * nodes] for q in range(chips)]
        whole = jnp.concatenate(pieces, axis=1)
        tops.append(whole[0:H])
        sums.append(whole[H : 2 * H])
    top = functools.reduce(jnp.maximum, tops)
    bottom = jnp.exp(-top)
    for own_top, own_sum in zip(tops, sums):
        bottom = bottom + own_sum * jnp.exp(own_top - top)
    factor = jnp.exp(tops[0] - top) / bottom
    shares = weight[...] * dot(factor, target_hit.astype(F32), exact=True)
    share[...] = shares
    wide = spread(shares)
    for r in range(R):
        scaled_rows[r] = (mixed[r].astype(F32) * wide).astype(BF)
    turn_back(table, scaled_rows, range(LMAX + 1), back)

    def collect(k):
        out = dot(target_hit, back[k], 1, 1).astype(BF)
        for p in range(chips):
            parts[p][k] = out[p * nodes : (p + 1) * nodes]

    each_k(collect)


def pull_kernel(chips, *refs):
    cots = refs[:chips]
    w_out, pack, table, mixed, share = refs[chips : chips + 5]
    pulled, pulled0, dalpha, dots = refs[chips + 5 : chips + 9]
    incoming, total_ref = refs[chips + 9 :]
    nodes = cots[0].shape[1]
    targets = chips * nodes
    target_hit = hits(pack[1:2], targets, BF)
    out_w = w_out[...]

    def gather(k):
        here = jnp.concatenate([c[k] for c in cots], axis=0)
        back = dot(out_w, here, 1, 1).astype(BF)
        incoming[k] = dot(back, target_hit).astype(BF)

    each_k(gather)
    total_ref[...] = jnp.zeros_like(total_ref)
    shares = share[...]
    wide_ref = pulled0
    wide_ref[...] = spread(shares)

    def emit(r, rows, lanes, total):
        total_ref[rows, lanes] += total * mixed[r, rows, lanes].astype(F32)
        pulled[r, rows, lanes] = (total * wide_ref[rows, lanes]).astype(BF)

    turn(table, incoming, range(LMAX + 1), emit)
    sums = head_sum(total_ref[...])
    dalpha[...] = sums
    dots[...] = dot(shares * sums, target_hit.astype(F32), 1, 1, exact=True)
    pulled0[...] = table[0, 0:1, :] * incoming[0].astype(F32) * wide_ref[...]


def back_kernel(chips, *refs):
    parts = refs[:chips]
    cots = refs[chips : 2 * chips]
    (feats_own, feats_sib, pulled, scaled, gating, table, pack, w_mix) = refs[2 * chips : 2 * chips + 8]
    (gate_sum, dv_own, dv_sib, g_mix, g_value, g_out) = refs[2 * chips + 8 : 2 * chips + 14]
    turned, spread_back = refs[2 * chips + 14 :]
    nodes = feats_own.shape[1]
    wide = H * VH
    gate = gating[...]
    zero = w_mix[0]
    gates = jnp.zeros_like(gate)
    grad = jnp.zeros((wide, wide), F32)
    for r in range(1, LMAX + 1):
        here = scaled[r]
        down = pulled[r]
        grad = grad + dot(here, down, 1, 1)
        out = dot(zero, down)
        gates = gates + out * here.astype(F32)
        turned[r] = (out * gate).astype(BF)
    g_mix[0] = grad
    for order in range(1, MMAX + 1):
        block = mix_block(w_mix, order, True)
        grad = jnp.zeros((2 * wide, 2 * wide), F32)
        for own, plus, minus in PAIRS:
            if own != order:
                continue
            down = jnp.concatenate([pulled[plus], pulled[minus]], axis=0)
            here = jnp.concatenate([scaled[plus], scaled[minus]], axis=0)
            grad = grad + dot(here, down, 1, 1)
            out = dot(block, down)
            prod = out * here.astype(F32)
            gates = gates + prod[:wide] + prod[wide:]
            turned[plus] = (out[:wide] * gate).astype(BF)
            turned[minus] = (out[wide:] * gate).astype(BF)
        g_mix[2 * order - 1] = grad[:wide, :wide] + grad[wide:, wide:]
        g_mix[2 * order] = grad[:wide, wide:] - grad[wide:, :wide]
    gate_sum[...] = gates
    turn_back(table, turned, range(1, LMAX + 1), spread_back)
    spread_back[0] = jnp.zeros_like(spread_back[0])
    source_hit = hits(pack[0:1], 2 * nodes, BF)

    def collect(k):
        out = dot(source_hit, spread_back[k], 1, 1).astype(BF)
        dv_own[k] = out[:nodes]
        dv_sib[k] = out[nodes:]

    each_k(collect)
    g_value[...] = jnp.zeros_like(g_value)
    g_out[...] = jnp.zeros_like(g_out)

    def weigh(i, carry):
        some = pl.ds(i * (LMAX + 1), LMAX + 1)

        def flat(ref):
            return ref[some].reshape((LMAX + 1) * nodes, wide)

        g_value[...] += dot(flat(feats_own), flat(dv_own), 0, 0) + dot(
            flat(feats_sib), flat(dv_sib), 0, 0
        )
        total = dot(flat(parts[0]), flat(cots[0]), 0, 0)
        for p in range(1, chips):
            total = total + dot(flat(parts[p]), flat(cots[p]), 0, 0)
        g_out[...] += total
        return carry

    lax.fori_loop(0, LMAX + 1, weigh, 0)


def tail_kernel(chips, *refs):
    dots = refs[:chips]
    firsts = refs[chips : 2 * chips]
    (
        feat0_sib,
        dalpha,
        share,
        pulled0,
        query,
        mixed0,
        scaled0,
        gating,
        table0,
        gate_sum,
        radial,
        pack,
        w_zero,
        g_mix,
        g_value,
        g_out,
    ) = refs[2 * chips : 2 * chips + 16]
    grads, dv_own, dv_sib, dquery = refs[2 * chips + 16 :]
    targets = dots[0].shape[1]
    nodes = targets // chips
    wide = H * VH
    target_hit = hits(pack[1:2], targets, F32)
    total = dots[0][...]
    for p in range(1, chips):
        pieces = [dots[p][:, (q ^ p) * nodes : ((q ^ p) + 1) * nodes] for q in range(chips)]
        total = total + jnp.concatenate(pieces, axis=1)
    dscore = share[...] * (dalpha[...] - dot(total, target_hit, exact=True))
    dlogit = spread(dscore) * (1.0 / VH**0.5)
    down = (pulled0[...] + dlogit * query[...]).astype(BF)
    here = scaled0[...]
    gate = gating[...]
    out = dot(w_zero[...], down)
    dgate = ((gate_sum[...] + out * here.astype(F32)) * (1.0 - gate)).astype(BF)
    back = (table0[0:1, :] * (out * gate).astype(BF).astype(F32)).astype(BF)
    source_hit = hits(pack[0:1], 2 * nodes, BF)
    dv = dot(source_hit, back, 1, 1).astype(BF)
    dv_own[...] = dv[:nodes]
    dv_sib[...] = dv[nodes:]
    dq = dot(target_hit, dlogit * mixed0[...].astype(F32), 1, 1, exact=True)
    dquery[...] = dq
    first = jnp.concatenate([f[...] for f in firsts], axis=0)
    node0 = jnp.concatenate([firsts[0][...], feat0_sib[...]], axis=0)
    grads[0:wide] = g_value[...] + dot(node0, dv, 0, 0)
    grads[wide : 2 * wide] = dot(first, dq.astype(BF), 0, 0)
    grads[2 * wide : 3 * wide] = g_out[...]
    grads[3 * wide : 4 * wide] = g_mix[0] + dot(here, down, 1, 1)
    for i in range(1, 2 * MMAX + 1):
        grads[(3 + i) * wide : (4 + i) * wide] = g_mix[i]
    at = (4 + 2 * MMAX) * wide
    grads[at:] = jnp.transpose(dot(dgate, radial[...]))


def nodes_kernel(chips, *refs):
    dqs = refs[:chips]
    dv_own, dv_sib, dv0_own, dv0_sib, cot, w_value, w_query, out = refs[chips:]
    value_w = w_value[...]

    def one(k):
        dv = (dv_own[k].astype(F32) + dv_sib[k].astype(F32)).astype(BF)
        out[k] = (cot[k].astype(F32) + dot(dv, value_w, 1, 1)).astype(BF)

    each_k(one)
    dv = (dv0_own[...].astype(F32) + dv0_sib[...].astype(F32)).astype(BF)
    dq = functools.reduce(jnp.add, [d[...] for d in dqs]).astype(BF)
    out[0] = (cot[0].astype(F32) + dot(dv, value_w, 1, 1) + dot(dq, w_query[...], 1, 1)).astype(BF)


def update_kernel(chips, *refs):
    parts = refs[:chips]
    feats, w_out, out = refs[chips:]
    out_w = w_out[...]

    def one(k):
        total = parts[0][k].astype(F32)
        for p in range(1, chips):
            total = total + parts[p][k].astype(F32)
        out[k] = (feats[k].astype(F32) + dot(total.astype(BF), out_w)).astype(BF)

    each_k(one)


def call(kernel, args, outs, scratch=(), smem=0, flops=0, limit=24):
    whole = pl.BlockSpec(memory_space=pltpu.VMEM)
    moved = sum(a.size * a.dtype.itemsize for a in args)
    moved += sum(int(np.prod(s)) * jnp.dtype(d).itemsize for s, d in outs)
    return pl.pallas_call(
        kernel,
        out_shape=[jax.ShapeDtypeStruct(s, d) for s, d in outs],
        in_specs=[pl.BlockSpec(memory_space=pltpu.SMEM)] * smem + [whole] * (len(args) - smem),
        out_specs=[whole] * len(outs),
        scratch_shapes=[pltpu.VMEM(s, d) for s, d in scratch],
        compiler_params=pltpu.CompilerParams(vmem_limit_bytes=limit << 20),
        cost_estimate=pl.CostEstimate(flops=flops, bytes_accessed=moved, transcendentals=0),
    )(*args)


def shards(
    node_feats,
    cotangent,
    sources,
    targets,
    bins,
    live_mask,
    radial,
    edge_bias,
    w_value,
    w_query,
    w_out,
    w_radial,
    w_mix,
    rotations,
):
    feats = jnp.transpose(node_feats[0], (1, 0, 2))
    cot = jnp.transpose(cotangent[0], (1, 0, 2))
    rot = jnp.transpose(rotations, (1, 2, 0))
    nodes = feats.shape[1]
    wide = feats.shape[2]
    slots = sources.shape[1]
    ranks = lax.axis_size("graph")
    planes = lax.axis_size("dp")
    chips = ranks // 2
    rank = lax.axis_index("graph")
    plane = lax.axis_index("dp")
    core, chip = rank % 2, rank // 2
    spot = chips * nodes

    def other_core(a):
        return lax.ppermute(a, "graph", [(i, i ^ 1) for i in range(ranks)])

    def along(a, step):
        return lax.ppermute(a, "graph", [(i, i ^ (2 * step)) for i in range(ranks)])

    def beside(a, step):
        return lax.ppermute(a, "dp", [(i, i ^ step) for i in range(planes)])

    def gathered(a):
        return [a] + [along(a, step) for step in range(1, chips)]

    ids = jnp.stack(
        [
            sources[0] - rank * nodes,
            ((targets[0] // (2 * nodes)) ^ chip) * nodes + targets[0] % nodes,
            bins[0],
            live_mask[0],
            *([jnp.zeros_like(bins[0])] * 4),
        ]
    )
    pack_own = jnp.concatenate([ids.astype(F32), jnp.transpose(edge_bias[0]).astype(F32)])
    bump = jnp.where(lax.broadcasted_iota(jnp.int32, pack_own.shape, 0) == 0, float(nodes), 0.0)
    pack_sib = other_core(pack_own + bump)
    radial_sib = other_core(radial[0])
    feats_sib = other_core(feats)
    firsts = gathered(feats[0])
    cots = gathered(cot)

    edge_f32 = ((wide, slots), F32)
    table, scaled, mixed, gating, pack, radial_here, weight, stats, query = call(
        functools.partial(lambda core_ref, *refs: forward_kernel(chips, core_ref, *refs)),
        [
            core.reshape(1),
            pack_own,
            pack_sib,
            radial[0],
            radial_sib,
            feats,
            feats_sib,
            *firsts,
            w_value,
            w_query,
            w_radial,
            w_mix,
            rot,
        ],
        [
            ((R, 56, slots), F32),
            ((R, wide, slots), BF),
            ((R, wide, slots), BF),
            edge_f32,
            ((16, slots), F32),
            ((slots, radial.shape[2]), BF),
            ((H, slots), F32),
            ((2 * H, spot), F32),
            edge_f32,
        ],
        [((K, wide, slots), BF)],
        smem=1,
        flops=4_000_000_000,
    )
    share, *parts = call(
        functools.partial(attend_kernel, chips),
        [*gathered(stats), weight, pack, table, mixed],
        [((H, slots), F32), *([((K, nodes, wide), BF)] * chips)],
        [((R, wide, slots), BF), ((K, wide, slots), BF)],
        flops=2_000_000_000,
    )
    arrived = [parts[0]] + [along(parts[step], step) for step in range(1, chips)]
    pulled, pulled0, dalpha, dots = call(
        functools.partial(pull_kernel, chips),
        [*cots, w_out, pack, table, mixed, share],
        [((R, wide, slots), BF), edge_f32, ((H, slots), F32), ((H, spot), F32)],
        [((K, wide, slots), BF), edge_f32],
        flops=2_000_000_000,
    )
    all_dots = gathered(dots)
    gate_sum, dv_own, dv_sib, g_mix, g_value, g_out = call(
        functools.partial(back_kernel, chips),
        [*parts, *cots, feats, feats_sib, pulled, scaled, gating, table, pack, w_mix],
        [
            edge_f32,
            ((K, nodes, wide), BF),
            ((K, nodes, wide), BF),
            (w_mix.shape, F32),
            ((wide, wide), F32),
            ((wide, wide), F32),
        ],
        [((R, wide, slots), BF), ((K, wide, slots), BF)],
        flops=4_000_000_000,
        limit=32,
    )
    dv_got = other_core(dv_sib)
    total_rows = (4 + 2 * MMAX) * wide + radial.shape[2]
    grads, dv0_own, dv0_sib, dquery = call(
        functools.partial(tail_kernel, chips),
        [
            *all_dots,
            *firsts,
            feats_sib[0],
            dalpha,
            share,
            pulled0,
            query,
            mixed[0],
            scaled[0],
            gating,
            table[0, 0:8],
            gate_sum,
            radial_here,
            pack,
            w_mix[0],
            g_mix,
            g_value,
            g_out,
        ],
        [
            ((total_rows, wide), F32),
            ((nodes, wide), BF),
            ((nodes, wide), BF),
            ((spot, wide), F32),
        ],
        flops=300_000_000,
    )

    halves = grads.reshape(2, total_rows // 2, wide)
    half = lax.dynamic_index_in_dim(halves, core, 0, False)
    half = half + other_core(
        lax.dynamic_index_in_dim(halves, 1 - core, 0, False).astype(BF)
    ).astype(F32)
    cut = half.reshape(planes, -1, wide)
    cut_b = cut.astype(BF)
    piece = lax.dynamic_index_in_dim(cut, plane, 0, False)
    for step in range(1, planes):
        piece = piece + beside(
            lax.dynamic_index_in_dim(cut_b, plane ^ step, 0, False), step
        ).astype(F32)
    sent = piece.astype(BF)
    for step in range(1, chips):
        piece = piece + along(sent, step).astype(F32)
    piece = piece.astype(BF)
    whole = jnp.zeros(cut.shape, BF)
    whole = lax.dynamic_update_index_in_dim(whole, piece, plane, 0)
    for step in range(1, planes):
        whole = lax.dynamic_update_index_in_dim(whole, beside(piece, step), plane ^ step, 0)
    mine = whole.reshape(-1, wide)
    theirs = other_core(mine)
    summed = jnp.where(
        core == 0, jnp.concatenate([mine, theirs]), jnp.concatenate([theirs, mine])
    ).astype(F32)

    dv0_got = other_core(dv0_sib)
    dq_blocks = dquery.reshape(chips, nodes, wide)
    dqs = [dq_blocks[0]] + [along(dq_blocks[step], step) for step in range(1, chips)]
    (grad_nodes,) = call(
        functools.partial(nodes_kernel, chips),
        [*dqs, dv_own, dv_got, dv0_own, dv0_got, cot, w_value, w_query],
        [((K, nodes, wide), BF)],
        flops=100_000_000,
    )
    (updated,) = call(
        functools.partial(update_kernel, chips),
        [*arrived, feats, w_out],
        [((K, nodes, wide), BF)],
        flops=100_000_000,
    )
    return (
        jnp.transpose(updated, (1, 0, 2))[None],
        jnp.transpose(grad_nodes, (1, 0, 2))[None],
        summed[0:wide],
        summed[wide : 2 * wide],
        summed[2 * wide : 3 * wide],
        summed[(4 + 2 * MMAX) * wide :],
        summed[3 * wide : (4 + 2 * MMAX) * wide].reshape(w_mix.shape),
    )


def solution(mesh):
    edge = P("dp", "graph")
    return jax.shard_map(
        shards,
        mesh=mesh,
        in_specs=(edge, edge, edge, edge, edge, edge, edge, edge, P(), P(), P(), P(), P(), P()),
        out_specs=(edge, edge, P(), P(), P(), P(), P()),
        check_vma=False,
    )
```

```python
import functools

import jax
import jax.numpy as jnp
import numpy as np
from jax import lax
from jax.experimental import pallas as pl
from jax.experimental.pallas import tpu as pltpu
from jax.sharding import PartitionSpec as P

H = 8
VH = 16
LMAX = 6
MMAX = 2
K = (LMAX + 1) ** 2
BF = jnp.bfloat16
F32 = jnp.float32
CHUNK = 16
LANES = 128


def frame_layout():
    index, degree_of = [], []
    for order in range(MMAX + 1):
        for sign in (1, -1) if order else (1,):
            for degree in range(order, LMAX + 1):
                index.append(degree * degree + degree + sign * order)
                degree_of.append(degree)
    return index, degree_of


ROWS, DEGREE = frame_layout()
R = len(ROWS)
OF_DEGREE = [[r for r in range(R) if DEGREE[r] == degree] for degree in range(LMAX + 1)]
PAIRS = []
_offset = LMAX + 1
for _order in range(1, MMAX + 1):
    _length = LMAX + 1 - _order
    for _i in range(_length):
        PAIRS.append((_order, _offset + _i, _offset + _length + _i))
    _offset += 2 * _length


def dot(a, b, ca=1, cb=0, exact=False):
    return lax.dot_general(
        a,
        b,
        (((ca,), (cb,)), ((), ())),
        precision=lax.Precision.HIGHEST if exact else None,
        preferred_element_type=F32,
    )


def flip(a):
    return jnp.transpose(a.astype(F32)).astype(a.dtype)


def hits(row, count, dtype):
    lines = lax.broadcasted_iota(jnp.int32, (count, row.shape[1]), 0)
    return jnp.where(lines == row.astype(jnp.int32), 1.0, 0.0).astype(dtype)


def head_sum(a):
    return jnp.sum(a.reshape(H, VH, a.shape[1]), axis=1)


def spread(a):
    return jnp.broadcast_to(a[:, None, :], (H, VH, a.shape[1])).reshape(H * VH, a.shape[1])


def turn(table, source, base, degrees, emit, finish=None):
    channels, edges = source.shape[1], source.shape[2]

    def step(i, carry):
        rows = pl.ds(pl.multiple_of(i * CHUNK, CHUNK), CHUNK)
        for start in range(0, edges, LANES):
            lanes = pl.ds(start, LANES)
            carried = None
            for degree in degrees:
                block = range(degree * degree, (degree + 1) ** 2)
                parts = [source[k, rows, lanes].astype(F32) for k in block]
                for r in OF_DEGREE[degree]:
                    total = None
                    for k, part in zip(block, parts):
                        at = base + start
                        term = table[r, k : k + 1, at : at + LANES] * part
                        total = term if total is None else total + term
                    carried = emit(r, rows, lanes, total, carried)
            if finish is not None:
                finish(rows, lanes, carried)
        return carry

    lax.fori_loop(0, channels // CHUNK, step, 0)


def turn_back(table, source, degrees, out):
    channels, edges = source.shape[1], source.shape[2]

    def step(i, carry):
        rows = pl.ds(pl.multiple_of(i * CHUNK, CHUNK), CHUNK)
        for start in range(0, edges, LANES):
            lanes = pl.ds(start, LANES)
            for degree in degrees:
                parts = [source[r, rows, lanes].astype(F32) for r in OF_DEGREE[degree]]
                for k in range(degree * degree, (degree + 1) ** 2):
                    total = None
                    for r, part in zip(OF_DEGREE[degree], parts):
                        term = table[r, k : k + 1, start : start + LANES] * part
                        total = term if total is None else total + term
                    out[k, rows, lanes] = total.astype(out.dtype)
        return carry

    lax.fori_loop(0, channels // CHUNK, step, 0)


def by_sevens(body):
    def step(i, carry):
        body(i * (LMAX + 1))
        return carry

    lax.fori_loop(0, LMAX + 1, step, 0)


def each_k(body):
    by_sevens(lambda k: [body(k + j) for j in range(LMAX + 1)] and None)


def rows_of(pieces):
    return jnp.concatenate(pieces, axis=0)


def whole_order(own, chips, p, span):
    return [own[:, (q ^ p) * span : ((q ^ p) + 1) * span] for q in range(chips)]


def mix_block(w_mix, order, back):
    even, odd = w_mix[2 * order - 1], w_mix[2 * order]
    if back:
        return jnp.concatenate(
            [
                jnp.concatenate([even, odd], axis=1),
                jnp.concatenate([-odd, even], axis=1),
            ],
            axis=0,
        )
    even, odd = flip(even), flip(odd)
    return jnp.concatenate(
        [
            jnp.concatenate([even, -odd], axis=1),
            jnp.concatenate([odd, even], axis=1),
        ],
        axis=0,
    )


def forward_kernel(chips, where, *refs):
    far = refs[:7]
    pack_own, pack_sib, radial_sib, feats_sib = refs[7:11]
    firsts = refs[11 : 11 + chips]
    refs = refs[11 + chips :]
    table, scaled, mixed, gating, pack, radial, weight, stats, query = refs[:9]
    parts = refs[9 : 9 + chips]
    incoming, scaled_rows, back = refs[9 + chips : 12 + chips]
    near = refs[12 + chips : 19 + chips]
    sems = refs[19 + chips]
    copies = [pltpu.make_async_copy(a, b, sems.at[i]) for i, (a, b) in enumerate(zip(far, near))]
    for c in copies:
        c.start()
    radial_own, w_radial, rot, feats_own, w_value, w_mix, w_query = near
    core, chip = where[0], where[1]
    slots = pack_own.shape[1]
    cap = slots // (2 * chips)
    nodes = feats_sib.shape[1]
    targets = chips * nodes
    bins = rot.shape[2]

    edge = lax.broadcasted_iota(jnp.int32, (2 * slots, slots), 1)
    place = lax.broadcasted_iota(jnp.int32, (2 * slots, slots), 0)
    side = (edge // cap) % 2
    origin = side * slots + (2 * ((edge // (2 * cap)) ^ chip) + core) * cap + edge % cap
    pick = jnp.where(place == origin, 1.0, 0.0).astype(BF)
    node_shift = jnp.where(
        (lax.broadcasted_iota(jnp.int32, (16, slots), 0) == 0), float(nodes), 0.0
    )
    packs = jnp.concatenate([pack_own[...], pack_sib[...] + node_shift], axis=1).astype(BF)
    rows = dot(packs, pick)
    lines = rows[4:5] * float(nodes) + rows[1:2]
    pack[...] = rows
    pack[1:2, :] = lines
    bin_hit = hits(rows[2:3], bins, BF)
    source_hit = hits(rows[0:1], 2 * nodes, BF)
    target_hit = hits(lines, targets, BF)
    for c in copies[:2]:
        c.wait()
    radial[...] = dot(pick, rows_of([radial_own[...], radial_sib[...]]), 0, 0).astype(BF)
    gating[...] = jax.nn.sigmoid(dot(flip(w_radial[...]), radial[...], 1, 1))
    copies[2].wait()
    for r, row in enumerate(ROWS):
        table[r, 0:K, :] = dot(rot[row], bin_hit)
    for c in copies[3:]:
        c.wait()
    value_t = flip(w_value[...])

    def gather(k):
        values = [
            dot(value_t, rows_of([feats_own[k + j], feats_sib[k + j]]), 1, 1).astype(BF)
            for j in range(LMAX + 1)
        ]
        got = dot(rows_of(values), source_hit).astype(BF)
        for j in range(LMAX + 1):
            incoming[k + j] = got[j * H * VH : (j + 1) * H * VH]

    by_sevens(gather)

    def emit(r, rows_, lanes, total, carried):
        gate = gating[rows_, lanes] if carried is None else carried
        scaled[r, rows_, lanes] = (total * gate).astype(BF)
        return gate

    turn(table, incoming, 0, range(LMAX + 1), emit)

    zero_t = flip(w_mix[0])
    for r in range(LMAX + 1):
        mixed[r] = dot(zero_t, scaled[r]).astype(BF)
    blocks = [None] + [mix_block(w_mix, order, False) for order in range(1, MMAX + 1)]
    for order, plus, minus in PAIRS:
        out = dot(blocks[order], rows_of([scaled[plus], scaled[minus]])).astype(BF)
        mixed[plus] = out[: H * VH]
        mixed[minus] = out[H * VH :]

    first = rows_of([f[...] for f in firsts])
    queries = dot(flip(w_query[...]), first, 1, 1).astype(BF)
    query[...] = dot(queries, target_hit)
    scores = head_sum(mixed[0].astype(F32) * query[...]) * (1.0 / VH**0.5) + rows[8:16]
    live = rows[3:4] > 0.5
    columns = jnp.transpose(pack[...])
    score_columns = jnp.transpose(scores)
    line = lax.broadcasted_iota(jnp.int32, (slots, targets), 1)
    chosen = (line == columns[:, 1:2].astype(jnp.int32)) & (columns[:, 3:4] > 0.5)
    top = jnp.concatenate(
        [
            jnp.max(jnp.where(chosen, score_columns[:, h : h + 1], 0.0), axis=0, keepdims=True)
            for h in range(H)
        ],
        axis=0,
    )
    top = jnp.maximum(top, 0.0)
    target_hit32 = target_hit.astype(F32)
    top_edge = dot(top, target_hit32, exact=True)
    weights = jnp.where(live, jnp.exp(jnp.where(live, scores - top_edge, 0.0)), 0.0)
    weight[...] = weights
    stats[0:H] = top
    stats[H : 2 * H] = dot(weights, target_hit32, 1, 1, exact=True)

    wide = spread(weights)
    for r in range(R):
        scaled_rows[r] = (mixed[r].astype(F32) * wide).astype(BF)
    turn_back(table, scaled_rows, range(LMAX + 1), back)

    def collect(k):
        out = dot(target_hit, back[k], 1, 1)
        for p in range(chips):
            parts[p][k] = out[p * nodes : (p + 1) * nodes].astype(parts[p].dtype)

    each_k(collect)


def pull_kernel(chips, second, *refs):
    some = chips // 2
    stats = refs[:chips]
    cots = refs[chips : chips + some]
    refs = refs[chips + some :]
    if second:
        before, refs = refs[0], refs[1:]
    else:
        raw, refs = refs[:chips], refs[chips:]
    w_out, pack, weight, table, mixed = refs[:5]
    pulled, pulled0, dalpha, share, dots = refs[5:10]
    parts, refs = ((), refs[10:]) if second else (refs[10 : 10 + chips], refs[10 + chips :])
    incoming, total_ref, wide_ref = refs
    nodes = cots[0].shape[1]
    edges = pulled.shape[2]
    base = edges if second else 0
    span = some * nodes
    lines = pack[1:2, base : base + edges] - (span if second else 0)
    target_hit = hits(lines, span, BF)
    target_hit32 = target_hit.astype(F32)
    out_w = w_out[...]

    def gather(k):
        backs = [
            dot(out_w, rows_of([c[k + j] for c in cots]), 1, 1).astype(BF) for j in range(LMAX + 1)
        ]
        got = dot(rows_of(backs), target_hit).astype(BF)
        for j in range(LMAX + 1):
            incoming[k + j] = got[j * H * VH : (j + 1) * H * VH]

    by_sevens(gather)

    wholes = [
        jnp.concatenate(whole_order(stats[p], chips, p, nodes), axis=1) for p in range(chips)
    ]
    top = functools.reduce(jnp.maximum, [w[0:H] for w in wholes])
    bottom = jnp.exp(-top)
    for w in wholes:
        bottom = bottom + w[H : 2 * H] * jnp.exp(w[0:H] - top)
    factor = jnp.exp(wholes[0][0:H] - top) / bottom
    mine = factor[:, (span if second else 0) : (2 * span if second else span)]
    shares = weight[:, base : base + edges] * dot(mine, target_hit32, exact=True)
    share[...] = shares
    wide_ref[...] = spread(shares)

    def emit(r, rows, lanes, total, carried):
        if carried is None:
            carried = (wide_ref[rows, lanes], None)
        wide, sums = carried
        far = pl.ds(base + lanes.start, lanes.size)
        term = total * mixed[r, rows, far].astype(F32)
        pulled[r, rows, lanes] = (total * wide).astype(BF)
        return (wide, term if sums is None else sums + term)

    def finish(rows, lanes, carried):
        total_ref[rows, lanes] = carried[1]

    turn(table, incoming, base, range(LMAX + 1), emit, finish)
    sums = head_sum(total_ref[...])
    dalpha[...] = sums
    here = dot(shares * sums, target_hit32, 1, 1, exact=True)
    if second:
        dots[...] = jnp.concatenate([before[...], here], axis=1)
    else:
        dots[...] = here
    pulled0[...] = table[0, 0:1, base : base + edges] * incoming[0].astype(F32) * wide_ref[...]
    if not second:
        scale = jnp.transpose(spread(factor))

        def normalize(k):
            for p in range(chips):
                parts[p][k] = (raw[p][k] * scale[p * nodes : (p + 1) * nodes]).astype(BF)

        each_k(normalize)


def back_kernel(chips, *refs):
    parts = refs[:chips]
    cots = refs[chips : 2 * chips]
    (feats_own, feats_sib, pulled_a, pulled_b, scaled, gating, table, pack, w_mix) = refs[
        2 * chips : 2 * chips + 9
    ]
    (gate_sum, dv_own, dv_sib, g_mix, g_value, g_out) = refs[2 * chips + 9 : 2 * chips + 15]
    turned, spread_back = refs[2 * chips + 15 :]
    nodes = feats_own.shape[1]
    wide = H * VH
    gate = gating[...]
    zero = w_mix[0]
    gates = jnp.zeros_like(gate)
    grad = jnp.zeros((wide, wide), F32)

    def pulled(r):
        return jnp.concatenate([pulled_a[r], pulled_b[r]], axis=1)

    for r in range(1, LMAX + 1):
        here = scaled[r]
        down = pulled(r)
        grad = grad + dot(here, down, 1, 1)
        out = dot(zero, down)
        gates = gates + out * here.astype(F32)
        turned[r] = (out * gate).astype(BF)
    g_mix[0] = grad
    for order in range(1, MMAX + 1):
        block = mix_block(w_mix, order, True)
        grad = jnp.zeros((2 * wide, 2 * wide), F32)
        for own, plus, minus in PAIRS:
            if own != order:
                continue
            down = rows_of([pulled(plus), pulled(minus)])
            here = rows_of([scaled[plus], scaled[minus]])
            grad = grad + dot(here, down, 1, 1)
            out = dot(block, down)
            prod = out * here.astype(F32)
            gates = gates + prod[:wide] + prod[wide:]
            turned[plus] = (out[:wide] * gate).astype(BF)
            turned[minus] = (out[wide:] * gate).astype(BF)
        g_mix[2 * order - 1] = grad[:wide, :wide] + grad[wide:, wide:]
        g_mix[2 * order] = grad[:wide, wide:] - grad[wide:, :wide]
    gate_sum[...] = gates
    turn_back(table, turned, range(1, LMAX + 1), spread_back)
    spread_back[0] = jnp.zeros_like(spread_back[0])
    source_hit = hits(pack[0:1], 2 * nodes, BF)

    def collect(k):
        out = dot(source_hit, spread_back[k], 1, 1).astype(BF)
        dv_own[k] = out[:nodes]
        dv_sib[k] = out[nodes:]

    each_k(collect)
    g_value[...] = jnp.zeros_like(g_value)
    g_out[...] = jnp.zeros_like(g_out)

    def weigh(k):
        some = pl.ds(k, LMAX + 1)

        def flat(ref):
            return ref[some].reshape((LMAX + 1) * nodes, wide)

        g_value[...] += dot(flat(feats_own), flat(dv_own), 0, 0) + dot(
            flat(feats_sib), flat(dv_sib), 0, 0
        )
        total = dot(flat(parts[0]), flat(cots[0]), 0, 0)
        for p in range(1, chips):
            total = total + dot(flat(parts[p]), flat(cots[p]), 0, 0)
        g_out[...] += total

    by_sevens(weigh)


def tail_kernel(chips, where, *refs):
    dots = refs[:chips]
    firsts = refs[chips : 2 * chips]
    refs = refs[2 * chips :]
    feat0_sib = refs[0]
    dalphas, shares, pulled0s = refs[1:3], refs[3:5], refs[5:7]
    query, mixed, scaled, gating, table, gate_sum, radial, pack, w_zero = refs[7:16]
    g_mix, g_value, g_out = refs[16:19]
    keep, send, dv_own = refs[19:22]
    dqs = refs[22 : 22 + chips]
    (grads,) = refs[22 + chips :]
    nodes = feat0_sib.shape[0]
    targets = chips * nodes
    wide = H * VH
    target_hit = hits(pack[1:2], targets, F32)

    def both(pair):
        return jnp.concatenate([pair[0][...], pair[1][...]], axis=1)

    total = dots[0][...]
    for p in range(1, chips):
        total = total + jnp.concatenate(whole_order(dots[p], chips, p, nodes), axis=1)
    dscore = both(shares) * (both(dalphas) - dot(total, target_hit, exact=True))
    dlogit = spread(dscore) * (1.0 / VH**0.5)
    down = (both(pulled0s) + dlogit * query[...]).astype(BF)
    here = scaled[0]
    gate = gating[...]
    out = dot(w_zero[...], down)
    dgate = ((gate_sum[...] + out * here.astype(F32)) * (1.0 - gate)).astype(BF)
    back = (table[0, 0:1, :] * (out * gate).astype(BF).astype(F32)).astype(BF)
    source_hit = hits(pack[0:1], 2 * nodes, BF)
    dv = dot(source_hit, back, 1, 1).astype(BF)
    dv_own[...] = dv[:nodes]
    dq = dot(target_hit, dlogit * mixed[0].astype(F32), 1, 1, exact=True)
    for p in range(chips):
        some = dq[p * nodes : (p + 1) * nodes]
        dqs[p][:nodes] = some.astype(BF)
        dqs[p][nodes:] = (some - some.astype(BF).astype(F32)).astype(BF)
    first = rows_of([f[...] for f in firsts])
    node0 = rows_of([firsts[0][...], feat0_sib[...]])
    pieces = [g_value[...] + dot(node0, dv, 0, 0), dot(first, dq.astype(BF), 0, 0), g_out[...]]
    pieces += [g_mix[0] + dot(here, down, 1, 1)]
    pieces += [g_mix[i] for i in range(1, 2 * MMAX + 1)]
    turned = dot(dgate, radial[...])
    for i in range(radial.shape[1] // wide):
        pieces.append(jnp.transpose(turned[:, i * wide : (i + 1) * wide]))
    half = grads.shape[1]
    for i, piece in enumerate(pieces):
        at = i * wide
        grads[at // half, at % half : at % half + wide] = piece
    keep[...] = grads[where[0]]
    send[: keep.shape[0]] = grads[1 - where[0]].astype(BF)
    send[keep.shape[0] :] = dv[nodes:]


def split_kernel(planes, where, keep, got, own, dv0, *outs):
    *sends, total = outs
    rows = keep.shape[0]
    total[...] = (keep[...] + got[:rows].astype(F32)).reshape(total.shape)
    dv0[...] = got[rows:]
    own[...] = total[where[1]]
    for step in range(1, planes):
        sends[step - 1][...] = total[where[1] ^ step].astype(BF)


def address_kernel(planes, own, *refs):
    got, refs = refs[: planes - 1], refs[planes - 1 :]
    dqs, outs = refs[: len(refs) // 2], refs[len(refs) // 2 :]
    total = functools.reduce(jnp.add, [own[...]] + [g[...].astype(F32) for g in got]).astype(BF)
    for dq, out in zip(dqs, outs):
        out[: own.shape[0]] = total
        out[own.shape[0] :] = dq[...]


def settle_kernel(*refs):
    *terms, piece, dquery = refs
    rows, nodes = piece.shape[0], dquery.shape[0]

    def total(values):
        while len(values) > 1:
            values = [a + b for a, b in zip(values[0::2], values[1::2])]
        return values[0].astype(BF)

    piece[...] = total([t[:rows].astype(F32) for t in terms])
    dquery[...] = total(
        [t[rows : rows + nodes].astype(F32) + t[rows + nodes :].astype(F32) for t in terms]
    )


def join_kernel(planes, where, *refs):
    mine, theirs = refs[:planes], refs[planes : 2 * planes]
    g_value, g_query, g_out, g_radial, g_mix, total = refs[2 * planes :]
    for step in range(planes):
        total[where[0] * planes + (where[1] ^ step)] = mine[step][...].astype(F32)
        total[(1 - where[0]) * planes + (where[1] ^ step)] = theirs[step][...].astype(F32)
    wide = H * VH
    flat = total[...].reshape(total.shape[0] * total.shape[1], wide)
    pieces = [flat[i * wide : (i + 1) * wide] for i in range(flat.shape[0] // wide)]
    g_value[...], g_query[...], g_out[...] = pieces[:3]
    for i in range(2 * MMAX + 1):
        g_mix[i] = pieces[3 + i]
    at = 4 + 2 * MMAX
    for i in range(g_radial.shape[0] // wide):
        g_radial[i * wide : (i + 1) * wide] = pieces[at + i]


def nodes_kernel(dquery, dv_own, dv_sib, dv0_own, dv0_sib, cot, w_value, w_query, out):
    value_w = w_value[...]

    def one(k):
        dv = (dv_own[k].astype(F32) + dv_sib[k].astype(F32)).astype(BF)
        out[k] = (cot[k].astype(F32) + dot(dv, value_w, 1, 1)).astype(BF)

    each_k(one)
    dv = (dv0_own[...].astype(F32) + dv0_sib[...].astype(F32)).astype(BF)
    query_part = dot(dquery[...], w_query[...], 1, 1)
    out[0] = (cot[0].astype(F32) + dot(dv, value_w, 1, 1) + query_part).astype(BF)


def add_kernel(*refs):
    *terms, out = refs

    def one(k):
        out[k] = functools.reduce(jnp.add, [t[k].astype(F32) for t in terms]).astype(BF)

    each_k(one)


def update_kernel(*refs):
    *parts, feats, w_out, out = refs
    out_w = w_out[...]

    def one(k):
        total = functools.reduce(jnp.add, [t[k].astype(F32) for t in parts])
        out[k] = (feats[k].astype(F32) + dot(total.astype(BF), out_w)).astype(BF)

    each_k(one)


def call(name, us, kernel, args, outs, scratch=(), smem=0, far=0, limit=24):
    whole = pl.BlockSpec(memory_space=pltpu.VMEM)
    specs = [pl.BlockSpec(memory_space=pltpu.SMEM)] * smem
    specs += [pl.BlockSpec(memory_space=pltpu.HBM)] * far
    specs += [whole] * (len(args) - smem - far)
    buffers = [pltpu.VMEM(s, d) for s, d in scratch]
    if far:
        buffers += [pltpu.VMEM(a.shape, a.dtype) for a in args[smem : smem + far]]
        buffers += [pltpu.SemaphoreType.DMA((far,))]
    return pl.pallas_call(
        kernel,
        out_shape=[jax.ShapeDtypeStruct(s, d) for s, d in outs],
        in_specs=specs,
        out_specs=[whole] * len(outs),
        scratch_shapes=buffers,
        compiler_params=pltpu.CompilerParams(vmem_limit_bytes=limit << 20),
        cost_estimate=pl.CostEstimate(
            flops=int(us * 1.15e9), bytes_accessed=1000, transcendentals=0
        ),
        name=name,
    )(*args)


def shards(
    node_feats,
    cotangent,
    sources,
    targets,
    bins,
    live_mask,
    radial,
    edge_bias,
    w_value,
    w_query,
    w_out,
    w_radial,
    w_mix,
    rotations,
):
    feats = jnp.transpose(node_feats[0], (1, 0, 2))
    cot = jnp.transpose(cotangent[0], (1, 0, 2))
    rot = jnp.transpose(rotations, (1, 2, 0))
    bias = jnp.transpose(edge_bias[0])
    nodes = feats.shape[1]
    wide = feats.shape[2]
    slots = sources.shape[1]
    ranks = lax.axis_size("graph")
    planes = lax.axis_size("dp")
    chips = ranks // 2
    some = chips // 2
    rank = lax.axis_index("graph")
    plane = lax.axis_index("dp")
    core, chip = rank % 2, rank // 2
    spot = chips * nodes
    where = jnp.stack([core, chip, plane]).astype(jnp.int32)
    where_sum = jnp.stack([core, plane]).astype(jnp.int32)

    def other_core(a):
        return lax.ppermute(a, "graph", [(i, i ^ 1) for i in range(ranks)])

    def along(a, step):
        return lax.ppermute(a, "graph", [(i, i ^ (2 * step)) for i in range(ranks)])

    def beside(a, step):
        return lax.ppermute(a, "dp", [(i, i ^ step) for i in range(planes)])

    def direct(a):
        return [a] + [along(a, step) for step in range(1, chips)]

    def doubled(a):
        have = {0: a}
        step = chips // 2
        while step:
            for p in list(have):
                have[p ^ step] = along(have[p], step)
            step //= 2
        return [have[p] for p in range(chips)]

    owner = targets // nodes
    line = lax.broadcasted_iota(jnp.int32, (16, slots), 0)
    ids = jnp.where(line == 0, sources - rank * nodes, 0)
    ids = jnp.where(line == 1, targets - owner * nodes, ids)
    ids = jnp.where(line == 2, bins, ids)
    ids = jnp.where(line == 3, live_mask, ids)
    ids = jnp.where(line == 4, (owner // 2) ^ chip, ids)
    pack_own = ids.astype(F32) + jnp.pad(bias.astype(F32), ((8, 0), (0, 0)))
    cots = doubled(cot)
    pack_sib = other_core(pack_own)
    radial_sib = other_core(radial[0])
    feats_sib = other_core(feats)
    firsts = direct(feats[0])

    edge_f32 = ((wide, slots), F32)
    half_f32 = ((wide, slots // 2), F32)
    block = ((K, nodes, wide), BF)
    table, scaled, mixed, gating, pack, radial_here, weight, stats, query, *raw = call(
        "forward",
        15,
        functools.partial(forward_kernel, chips),
        [
            where,
            radial[0],
            w_radial,
            rot,
            feats,
            w_value,
            w_mix,
            w_query,
            pack_own,
            pack_sib,
            radial_sib,
            feats_sib,
            *firsts,
        ],
        [
            ((R, 56, slots), F32),
            ((R, wide, slots), BF),
            ((R, wide, slots), BF),
            edge_f32,
            ((16, slots), F32),
            ((slots, radial.shape[2]), BF),
            ((H, slots), F32),
            ((2 * H, spot), F32),
            edge_f32,
            *([((K, nodes, wide), F32)] * chips),
        ],
        [((K, wide, slots), BF), ((R, wide, slots), BF), ((K, wide, slots), BF)],
        smem=1,
        far=7,
        limit=32,
    )
    all_stats = direct(stats)

    def pull(second, extra):
        mine = slice(some, chips) if second else slice(0, some)
        return call(
        "pull",
        4.5,
            functools.partial(pull_kernel, chips, second),
            [*all_stats, *cots[mine], *extra, w_out, pack, weight, table, mixed],
            [
                ((R, wide, slots // 2), BF),
                half_f32,
                ((H, slots // 2), F32),
                ((H, slots // 2), F32),
                ((H, spot if second else spot // 2), F32),
                *([] if second else [block] * chips),
            ],
            [((K, wide, slots // 2), BF), half_f32, half_f32],
        )

    pulled_a, pulled0_a, dalpha_a, share_a, dots_a, *parts = pull(False, raw)

    parts, cots[-1] = lax.optimization_barrier((parts, cots[-1]))
    pending = {p: [parts[p]] for p in range(chips)}
    near = {p: along(parts[p], 1) for p in range(chips) if p & 1}
    pulled_b, pulled0_b, dalpha_b, share_b, dots = pull(True, [dots_a])
    all_dots = direct(dots)
    for p, got in near.items():
        del pending[p]
        pending[p ^ 1].append(got)
    summed = {}
    for p in pending:
        if p:
            (summed[p],) = call("add", 1, add_kernel, pending[p], [block])
    summed, pulled_b = lax.optimization_barrier((summed, pulled_b))
    step = 2
    while step < chips:
        for p in [p for p in summed if p & step]:
            got = along(summed.pop(p), step)
            if p ^ step:
                (summed[p ^ step],) = call("add", 1, add_kernel, [summed[p ^ step], got], [block])
            else:
                pending[0].append(got)
        step *= 2
    gate_sum, dv_own, dv_sib, g_mix, g_value, g_out = call(
        "back",
        7.5,
        functools.partial(back_kernel, chips),
        [*parts, *cots, feats, feats_sib, pulled_a, pulled_b, scaled, gating, table, pack, w_mix],
        [edge_f32, block, block, (w_mix.shape, F32), ((wide, wide), F32), ((wide, wide), F32)],
        [((R, wide, slots), BF), ((K, wide, slots), BF)],
        limit=32,
    )
    dv_got = other_core(dv_sib)

    total_rows = (4 + 2 * MMAX) * wide + radial.shape[2]
    cut = total_rows // (2 * planes)
    small = ((nodes, wide), BF)
    keep, send, dv0_own, *dqs = call(
        "tail",
        1.8,
        functools.partial(tail_kernel, chips),
        [
            where_sum,
            *all_dots,
            *firsts,
            feats_sib[0],
            dalpha_a,
            dalpha_b,
            share_a,
            share_b,
            pulled0_a,
            pulled0_b,
            query,
            mixed,
            scaled,
            gating,
            table,
            gate_sum,
            radial_here,
            pack,
            w_mix[0],
            g_mix,
            g_value,
            g_out,
        ],
        [
            ((total_rows // 2, wide), F32),
            ((total_rows // 2 + nodes, wide), BF),
            small,
            *([((2 * nodes, wide), BF)] * chips),
        ],
        [((2, total_rows // 2, wide), F32)],
        smem=1,
    )

    got = other_core(send)
    own, dv0_got, *sends = call(
        "split",
        0.6,
        functools.partial(split_kernel, planes),
        [where_sum, keep, got],
        [((cut, wide), F32), small, *([((cut, wide), BF)] * (planes - 1))],
        [((planes, cut, wide), F32)],
        smem=1,
    )
    got = [beside(sends[step - 1], step) for step in range(1, planes)]
    got, pending[0][1] = lax.optimization_barrier((got, pending[0][1]))
    letters = call(
        "address",
        0.6,
        functools.partial(address_kernel, planes),
        [own, *got, *dqs],
        [((cut + 2 * nodes, wide), BF)] * chips,
    )
    terms = [letters[0]] + [along(letters[step], step) for step in range(1, chips)]
    terms, pending[0] = lax.optimization_barrier((terms, pending[0]))
    piece, dquery = call("settle", 0.6, settle_kernel, terms, [((cut, wide), BF), small])
    (updated,) = call("update", 2, update_kernel, [*pending[0], feats, w_out], [block])
    mine = [piece] + [beside(piece, step) for step in range(1, planes)]
    theirs = [other_core(a) for a in mine]
    grads = call(
        "join",
        1.5,
        functools.partial(join_kernel, planes),
        [where_sum, *mine, *theirs],
        [
            ((wide, wide), F32),
            ((wide, wide), F32),
            ((wide, wide), F32),
            ((radial.shape[2], wide), F32),
            (w_mix.shape, F32),
        ],
        [((2 * planes, cut, wide), F32)],
        smem=1,
    )

    (grad_nodes,) = call(
        "nodes",
        2.6,
        nodes_kernel,
        [dquery, dv_own, dv_got, dv0_own, dv0_got, cot, w_value, w_query],
        [block],
    )
    return (
        jnp.transpose(updated, (1, 0, 2))[None],
        jnp.transpose(grad_nodes, (1, 0, 2))[None],
        *grads,
    )


def solution(mesh):
    edge = P("dp", "graph")
    return jax.shard_map(
        shards,
        mesh=mesh,
        in_specs=(edge, edge, edge, edge, edge, edge, edge, edge, P(), P(), P(), P(), P(), P()),
        out_specs=(edge, edge, P(), P(), P(), P(), P()),
        check_vma=False,
    )
```

```python
import functools

import jax
import jax.numpy as jnp
import numpy as np
from jax import lax
from jax.experimental import pallas as pl
from jax.experimental.pallas import tpu as pltpu
from jax.sharding import PartitionSpec as P

H = 8
VH = 16
LMAX = 6
MMAX = 2
K = (LMAX + 1) ** 2
BF = jnp.bfloat16
F32 = jnp.float32
CHUNK = 16
LANES = 128


def frame_layout():
    index, degree_of = [], []
    for order in range(MMAX + 1):
        for sign in (1, -1) if order else (1,):
            for degree in range(order, LMAX + 1):
                index.append(degree * degree + degree + sign * order)
                degree_of.append(degree)
    return index, degree_of


ROWS, DEGREE = frame_layout()
R = len(ROWS)
OF_DEGREE = [[r for r in range(R) if DEGREE[r] == degree] for degree in range(LMAX + 1)]
PAIRS = []
_offset = LMAX + 1
for _order in range(1, MMAX + 1):
    _length = LMAX + 1 - _order
    for _i in range(_length):
        PAIRS.append((_order, _offset + _i, _offset + _length + _i))
    _offset += 2 * _length


def dot(a, b, ca=1, cb=0, exact=False):
    return lax.dot_general(
        a,
        b,
        (((ca,), (cb,)), ((), ())),
        precision=lax.Precision.HIGHEST if exact else None,
        preferred_element_type=F32,
    )


def flip(a):
    return jnp.transpose(a.astype(F32)).astype(a.dtype)


def hits(row, count, dtype):
    lines = lax.broadcasted_iota(jnp.int32, (count, row.shape[1]), 0)
    return jnp.where(lines == row.astype(jnp.int32), 1.0, 0.0).astype(dtype)


def head_sum(a):
    return jnp.sum(a.reshape(H, VH, a.shape[1]), axis=1)


def spread(a):
    return jnp.broadcast_to(a[:, None, :], (H, VH, a.shape[1])).reshape(H * VH, a.shape[1])


def turn(table, source, base, degrees, emit, finish=None):
    channels, edges = source.shape[1], source.shape[2]

    def step(i, carry):
        rows = pl.ds(pl.multiple_of(i * CHUNK, CHUNK), CHUNK)
        for start in range(0, edges, LANES):
            lanes = pl.ds(start, LANES)
            carried = None
            for degree in degrees:
                block = range(degree * degree, (degree + 1) ** 2)
                parts = [source[k, rows, lanes].astype(F32) for k in block]
                for r in OF_DEGREE[degree]:
                    total = None
                    for k, part in zip(block, parts):
                        at = base + start
                        term = table[r, k : k + 1, at : at + LANES] * part
                        total = term if total is None else total + term
                    carried = emit(r, rows, lanes, total, carried)
            if finish is not None:
                finish(rows, lanes, carried)
        return carry

    lax.fori_loop(0, channels // CHUNK, step, 0)


def turn_back(table, source, degrees, out):
    channels, edges = source.shape[1], source.shape[2]

    def step(i, carry):
        rows = pl.ds(pl.multiple_of(i * CHUNK, CHUNK), CHUNK)
        for start in range(0, edges, LANES):
            lanes = pl.ds(start, LANES)
            for degree in degrees:
                parts = [source[r, rows, lanes].astype(F32) for r in OF_DEGREE[degree]]
                for k in range(degree * degree, (degree + 1) ** 2):
                    total = None
                    for r, part in zip(OF_DEGREE[degree], parts):
                        term = table[r, k : k + 1, start : start + LANES] * part
                        total = term if total is None else total + term
                    out[k, rows, lanes] = total.astype(out.dtype)
        return carry

    lax.fori_loop(0, channels // CHUNK, step, 0)


def by_sevens(body):
    def step(i, carry):
        body(i * (LMAX + 1))
        return carry

    lax.fori_loop(0, LMAX + 1, step, 0)


def each_k(body):
    by_sevens(lambda k: [body(k + j) for j in range(LMAX + 1)] and None)


def rows_of(pieces):
    return jnp.concatenate(pieces, axis=0)


def whole_order(own, chips, p, span):
    return [own[:, (q ^ p) * span : ((q ^ p) + 1) * span] for q in range(chips)]


def mix_block(w_mix, order, back):
    even, odd = w_mix[2 * order - 1], w_mix[2 * order]
    if back:
        return jnp.concatenate(
            [
                jnp.concatenate([even, odd], axis=1),
                jnp.concatenate([-odd, even], axis=1),
            ],
            axis=0,
        )
    even, odd = flip(even), flip(odd)
    return jnp.concatenate(
        [
            jnp.concatenate([even, -odd], axis=1),
            jnp.concatenate([odd, even], axis=1),
        ],
        axis=0,
    )


def forward_kernel(chips, where, *refs):
    far, refs = refs[:6], refs[6:]
    pack_own, pack_sib, radial_sib, feats_sib, *refs = refs
    table, scaled, mixed, gating, pack, radial, incoming, *refs = refs
    near, sems = refs[:6], refs[6]
    copies = [pltpu.make_async_copy(a, b, sems.at[i]) for i, (a, b) in enumerate(zip(far, near))]
    for c in copies:
        c.start()
    radial_own, w_radial, rot, feats_own, w_value, w_mix = near
    core, chip = where[0], where[1]
    slots = pack_own.shape[1]
    cap = slots // (2 * chips)
    nodes = feats_sib.shape[1]
    bins = rot.shape[2]

    edge = lax.broadcasted_iota(jnp.int32, (2 * slots, slots), 1)
    place = lax.broadcasted_iota(jnp.int32, (2 * slots, slots), 0)
    side = (edge // cap) % 2
    origin = side * slots + (2 * ((edge // (2 * cap)) ^ chip) + core) * cap + edge % cap
    pick = jnp.where(place == origin, 1.0, 0.0).astype(BF)

    def relative(raw):
        ids = raw[0:2].astype(jnp.int32)
        owner = ids[1:2] // nodes
        source = ids[0:1] - 2 * chip * nodes
        swapped = jnp.where(source < nodes, source + nodes, source - nodes)
        rows_ = [jnp.where(core == 0, source, swapped), ids[1:2] - owner * nodes]
        rows_ = [a.astype(F32) for a in rows_ + [(owner // 2) ^ chip]]
        return jnp.concatenate([rows_[0], rows_[1], raw[2:4], rows_[2], raw[5:]], axis=0)

    packs = [relative(pack_own[...]), relative(pack_sib[...])]
    packs = jnp.concatenate(packs, axis=1).astype(BF)
    rows = dot(packs, pick)
    lines = rows[4:5] * float(nodes) + rows[1:2]
    pack[...] = rows
    pack[1:2, :] = lines
    bin_hit = hits(rows[2:3], bins, BF)
    source_hit = hits(rows[0:1], 2 * nodes, BF)
    for c in copies[:2]:
        c.wait()
    radial[...] = dot(pick, rows_of([radial_own[...], radial_sib[...]]), 0, 0).astype(BF)
    gating[...] = jax.nn.sigmoid(dot(flip(w_radial[...]), radial[...], 1, 1))
    copies[2].wait()
    for r, row in enumerate(ROWS):
        table[r, 0:K, :] = dot(rot[row], bin_hit)
    for c in copies[3:]:
        c.wait()
    value_t = flip(w_value[...])

    def gather(k):
        values = [
            dot(value_t, rows_of([feats_own[k + j], feats_sib[k + j]]), 1, 1).astype(BF)
            for j in range(LMAX + 1)
        ]
        got = dot(rows_of(values), source_hit).astype(BF)
        for j in range(LMAX + 1):
            incoming[k + j] = got[j * H * VH : (j + 1) * H * VH]

    by_sevens(gather)

    def emit(r, rows_, lanes, total, carried):
        gate = gating[rows_, lanes] if carried is None else carried
        scaled[r, rows_, lanes] = (total * gate).astype(BF)
        return gate

    turn(table, incoming, 0, range(LMAX + 1), emit)

    zero_t = flip(w_mix[0])
    for r in range(LMAX + 1):
        mixed[r] = dot(zero_t, scaled[r]).astype(BF)
    blocks = [None] + [mix_block(w_mix, order, False) for order in range(1, MMAX + 1)]
    for order, plus, minus in PAIRS:
        out = dot(blocks[order], rows_of([scaled[plus], scaled[minus]])).astype(BF)
        mixed[plus] = out[: H * VH]
        mixed[minus] = out[H * VH :]


def attend_kernel(chips, *refs):
    far, refs = refs[0], refs[1:]
    firsts, refs = refs[:chips], refs[chips:]
    pack, table, mixed, weight, stats, query, *refs = refs
    parts, refs = refs[:chips], refs[chips:]
    scaled_rows, back, w_query, sems = refs
    copy = pltpu.make_async_copy(far, w_query, sems.at[0])
    copy.start()
    slots = pack.shape[1]
    nodes = firsts[0].shape[0]
    targets = chips * nodes
    rows = pack[...]
    target_hit = hits(rows[1:2], targets, BF)
    first = rows_of([f[...] for f in firsts])
    copy.wait()
    queries = dot(flip(w_query[...]), first, 1, 1).astype(BF)
    query[...] = dot(queries, target_hit)
    scores = head_sum(mixed[0].astype(F32) * query[...]) * (1.0 / VH**0.5) + rows[8:16]
    live = rows[3:4] > 0.5
    columns = jnp.transpose(rows)
    score_columns = jnp.transpose(scores)
    line = lax.broadcasted_iota(jnp.int32, (slots, targets), 1)
    chosen = (line == columns[:, 1:2].astype(jnp.int32)) & (columns[:, 3:4] > 0.5)
    top = jnp.concatenate(
        [
            jnp.max(jnp.where(chosen, score_columns[:, h : h + 1], 0.0), axis=0, keepdims=True)
            for h in range(H)
        ],
        axis=0,
    )
    top = jnp.maximum(top, 0.0)
    target_hit32 = target_hit.astype(F32)
    top_edge = dot(top, target_hit32, exact=True)
    weights = jnp.where(live, jnp.exp(jnp.where(live, scores - top_edge, 0.0)), 0.0)
    weight[...] = weights
    stats[0:H] = top
    stats[H : 2 * H] = dot(weights, target_hit32, 1, 1, exact=True)

    wide = spread(weights)
    for r in range(R):
        scaled_rows[r] = (mixed[r].astype(F32) * wide).astype(BF)
    turn_back(table, scaled_rows, range(LMAX + 1), back)

    def collect(k):
        out = dot(target_hit, back[k], 1, 1)
        for p in range(chips):
            parts[p][k] = out[p * nodes : (p + 1) * nodes].astype(parts[p].dtype)

    each_k(collect)


def share_kernel(chips, *refs):
    stats, raw = refs[:chips], refs[chips : 2 * chips]
    weight, pack, share = refs[2 * chips : 2 * chips + 3]
    parts = refs[2 * chips + 3 :]
    targets = stats[0].shape[1]
    nodes = targets // chips
    target_hit32 = hits(pack[1:2], targets, F32)
    wholes = [
        jnp.concatenate(whole_order(stats[p], chips, p, nodes), axis=1) for p in range(chips)
    ]
    top = functools.reduce(jnp.maximum, [w[0:H] for w in wholes])
    bottom = jnp.exp(-top)
    for w in wholes:
        bottom = bottom + w[H : 2 * H] * jnp.exp(w[0:H] - top)
    factor = jnp.exp(wholes[0][0:H] - top) / bottom
    share[...] = weight[...] * dot(factor, target_hit32, exact=True)
    scale = jnp.transpose(spread(factor))

    def normalize(k):
        for p in range(chips):
            parts[p][k] = (raw[p][k] * scale[p * nodes : (p + 1) * nodes]).astype(BF)

    each_k(normalize)


def pull_kernel(chips, second, *refs):
    some = chips // 2
    cots, refs = refs[:some], refs[some:]
    w_out, pack, table, mixed, *refs = refs
    if second:
        before, share, pulled, pulled0, dalpha, dots, *refs = refs
    else:
        pulled, pulled0, dalpha, *refs = refs
    incoming, total_ref = refs
    nodes = cots[0].shape[1]
    edges = pulled.shape[2]
    base = edges if second else 0
    span = some * nodes
    lines = pack[1:2, base : base + edges] - (span if second else 0)
    target_hit = hits(lines, span, BF)
    out_w = w_out[...]

    def gather(k):
        backs = [
            dot(out_w, rows_of([c[k + j] for c in cots]), 1, 1).astype(BF) for j in range(LMAX + 1)
        ]
        got = dot(rows_of(backs), target_hit).astype(BF)
        for j in range(LMAX + 1):
            incoming[k + j] = got[j * H * VH : (j + 1) * H * VH]

    by_sevens(gather)

    def emit(r, rows, lanes, total, carried):
        far = pl.ds(base + lanes.start, lanes.size)
        term = total * mixed[r, rows, far].astype(F32)
        pulled[r, rows, lanes] = total.astype(BF)
        return term if carried is None else carried + term

    def finish(rows, lanes, carried):
        total_ref[rows, lanes] = carried

    turn(table, incoming, base, range(LMAX + 1), emit, finish)
    sums = head_sum(total_ref[...])
    dalpha[...] = sums
    pulled0[...] = table[0, 0:1, base : base + edges] * incoming[0].astype(F32)
    if second:
        every = share[...] * jnp.concatenate([before[...], sums], axis=1)
        target_hit32 = hits(pack[1:2], dots.shape[1], F32)
        dots[...] = dot(every, target_hit32, 1, 1, exact=True)


def back_kernel(chips, *refs):
    parts = refs[:chips]
    cots = refs[chips : 2 * chips]
    (feats_own, feats_sib, pulled_a, pulled_b, share, scaled, gating, table, pack, w_mix) = refs[
        2 * chips : 2 * chips + 10
    ]
    (gate_sum, dv_own, dv_sib, g_mix, g_value, g_out) = refs[2 * chips + 10 : 2 * chips + 16]
    turned, spread_back = refs[2 * chips + 16 :]
    nodes = feats_own.shape[1]
    wide = H * VH
    gate = gating[...]
    zero = w_mix[0]
    shares = spread(share[...])
    gates = jnp.zeros_like(gate)
    grad = jnp.zeros((wide, wide), F32)

    def pulled(r):
        whole = jnp.concatenate([pulled_a[r], pulled_b[r]], axis=1)
        return (whole.astype(F32) * shares).astype(BF)

    for r in range(1, LMAX + 1):
        here = scaled[r]
        down = pulled(r)
        grad = grad + dot(here, down, 1, 1)
        out = dot(zero, down)
        gates = gates + out * here.astype(F32)
        turned[r] = (out * gate).astype(BF)
    g_mix[0] = grad
    for order in range(1, MMAX + 1):
        block = mix_block(w_mix, order, True)
        grad = jnp.zeros((2 * wide, 2 * wide), F32)
        for own, plus, minus in PAIRS:
            if own != order:
                continue
            down = rows_of([pulled(plus), pulled(minus)])
            here = rows_of([scaled[plus], scaled[minus]])
            grad = grad + dot(here, down, 1, 1)
            out = dot(block, down)
            prod = out * here.astype(F32)
            gates = gates + prod[:wide] + prod[wide:]
            turned[plus] = (out[:wide] * gate).astype(BF)
            turned[minus] = (out[wide:] * gate).astype(BF)
        g_mix[2 * order - 1] = grad[:wide, :wide] + grad[wide:, wide:]
        g_mix[2 * order] = grad[:wide, wide:] - grad[wide:, :wide]
    gate_sum[...] = gates
    turn_back(table, turned, range(1, LMAX + 1), spread_back)
    spread_back[0] = jnp.zeros_like(spread_back[0])
    source_hit = hits(pack[0:1], 2 * nodes, BF)

    def collect(k):
        out = dot(source_hit, spread_back[k], 1, 1).astype(BF)
        dv_own[k] = out[:nodes]
        dv_sib[k] = out[nodes:]

    each_k(collect)
    g_value[...] = jnp.zeros_like(g_value)
    g_out[...] = jnp.zeros_like(g_out)

    def weigh(k):
        some = pl.ds(k, LMAX + 1)

        def flat(ref):
            return ref[some].reshape((LMAX + 1) * nodes, wide)

        g_value[...] += dot(flat(feats_own), flat(dv_own), 0, 0) + dot(
            flat(feats_sib), flat(dv_sib), 0, 0
        )
        total = dot(flat(parts[0]), flat(cots[0]), 0, 0)
        for p in range(1, chips):
            total = total + dot(flat(parts[p]), flat(cots[p]), 0, 0)
        g_out[...] += total

    by_sevens(weigh)


def tail_kernel(chips, where, *refs):
    dots = refs[:chips]
    firsts = refs[chips : 2 * chips]
    refs = refs[2 * chips :]
    feats_sib = refs[0]
    dalphas, share, pulled0s = refs[1:3], refs[3], refs[4:6]
    query, mixed, scaled, gating, table, gate_sum, radial, pack, w_mix = refs[6:15]
    g_mix, g_value, g_out = refs[15:18]
    keep, send, dv_own = refs[18:21]
    dqs = refs[21 : 21 + chips]
    (grads,) = refs[21 + chips :]
    nodes = feats_sib.shape[1]
    targets = chips * nodes
    wide = H * VH
    target_hit = hits(pack[1:2], targets, F32)

    def both(pair):
        return jnp.concatenate([pair[0][...], pair[1][...]], axis=1)

    total = dots[0][...]
    for p in range(1, chips):
        total = total + jnp.concatenate(whole_order(dots[p], chips, p, nodes), axis=1)
    dscore = share[...] * (both(dalphas) - dot(total, target_hit, exact=True))
    dlogit = spread(dscore) * (1.0 / VH**0.5)
    pulled0 = both(pulled0s) * spread(share[...])
    down = (pulled0 + dlogit * query[...]).astype(BF)
    here = scaled[0]
    gate = gating[...]
    out = dot(w_mix[0], down)
    dgate = ((gate_sum[...] + out * here.astype(F32)) * (1.0 - gate)).astype(BF)
    back = (table[0, 0:1, :] * (out * gate).astype(BF).astype(F32)).astype(BF)
    source_hit = hits(pack[0:1], 2 * nodes, BF)
    dv = dot(source_hit, back, 1, 1).astype(BF)
    dv_own[...] = dv[:nodes]
    dq = dot(target_hit, dlogit * mixed[0].astype(F32), 1, 1, exact=True)
    for p in range(chips):
        some = dq[p * nodes : (p + 1) * nodes]
        dqs[p][:nodes] = some.astype(BF)
        dqs[p][nodes:] = (some - some.astype(BF).astype(F32)).astype(BF)
    first = rows_of([f[...] for f in firsts])
    node0 = rows_of([firsts[0][...], feats_sib[0]])
    pieces = [g_value[...] + dot(node0, dv, 0, 0), dot(first, dq.astype(BF), 0, 0), g_out[...]]
    pieces += [g_mix[0] + dot(here, down, 1, 1)]
    pieces += [g_mix[i] for i in range(1, 2 * MMAX + 1)]
    turned = dot(dgate, radial[...])
    for i in range(radial.shape[1] // wide):
        pieces.append(jnp.transpose(turned[:, i * wide : (i + 1) * wide]))
    half = grads.shape[1]
    for i, piece in enumerate(pieces):
        at = i * wide
        grads[at // half, at % half : at % half + wide] = piece
    keep[...] = grads[where[0]]
    send[: keep.shape[0]] = grads[1 - where[0]].astype(BF)
    send[keep.shape[0] :] = dv[nodes:]


def split_kernel(planes, where, keep, got, own, dv0, *outs):
    *sends, total = outs
    rows = keep.shape[0]
    total[...] = (keep[...] + got[:rows].astype(F32)).reshape(total.shape)
    dv0[...] = got[rows:]
    own[...] = total[where[1]]
    for step in range(1, planes):
        sends[step - 1][...] = total[where[1] ^ step].astype(BF)


def address_kernel(planes, own, *refs):
    got, refs = refs[: planes - 1], refs[planes - 1 :]
    dqs, outs = refs[: len(refs) // 2], refs[len(refs) // 2 :]
    total = functools.reduce(jnp.add, [own[...]] + [g[...].astype(F32) for g in got]).astype(BF)
    for dq, out in zip(dqs, outs):
        out[: own.shape[0]] = total
        out[own.shape[0] :] = dq[...]


def settle_kernel(*refs):
    *terms, piece, dquery = refs
    rows, nodes = piece.shape[0], dquery.shape[0]

    def total(values):
        while len(values) > 1:
            values = [a + b for a, b in zip(values[0::2], values[1::2])]
        return values[0].astype(BF)

    piece[...] = total([t[:rows].astype(F32) for t in terms])
    dquery[...] = total(
        [t[rows : rows + nodes].astype(F32) + t[rows + nodes :].astype(F32) for t in terms]
    )


def join_kernel(planes, where, *refs):
    mine, theirs = refs[:planes], refs[planes : 2 * planes]
    g_value, g_query, g_out, g_radial, g_mix, total = refs[2 * planes :]
    for step in range(planes):
        total[where[0] * planes + (where[1] ^ step)] = mine[step][...].astype(F32)
        total[(1 - where[0]) * planes + (where[1] ^ step)] = theirs[step][...].astype(F32)
    wide = H * VH
    flat = total[...].reshape(total.shape[0] * total.shape[1], wide)
    pieces = [flat[i * wide : (i + 1) * wide] for i in range(flat.shape[0] // wide)]
    g_value[...], g_query[...], g_out[...] = pieces[:3]
    for i in range(2 * MMAX + 1):
        g_mix[i] = pieces[3 + i]
    at = 4 + 2 * MMAX
    for i in range(g_radial.shape[0] // wide):
        g_radial[i * wide : (i + 1) * wide] = pieces[at + i]


def nodes_kernel(dquery, dv_own, dv_sib, dv0_own, dv0_sib, cot, w_value, w_query, out):
    value_w = w_value[...]

    def one(k):
        dv = (dv_own[k].astype(F32) + dv_sib[k].astype(F32)).astype(BF)
        out[k] = (cot[k].astype(F32) + dot(dv, value_w, 1, 1)).astype(BF)

    each_k(one)
    dv = (dv0_own[...].astype(F32) + dv0_sib[...].astype(F32)).astype(BF)
    query_part = dot(dquery[...], w_query[...], 1, 1)
    out[0] = (cot[0].astype(F32) + dot(dv, value_w, 1, 1) + query_part).astype(BF)


def add_kernel(*refs):
    *terms, out = refs

    def one(k):
        out[k] = functools.reduce(jnp.add, [t[k].astype(F32) for t in terms]).astype(BF)

    each_k(one)


def update_kernel(*refs):
    *parts, feats, w_out, out = refs
    out_w = w_out[...]

    def one(k):
        total = functools.reduce(jnp.add, [t[k].astype(F32) for t in parts])
        out[k] = (feats[k].astype(F32) + dot(total.astype(BF), out_w)).astype(BF)

    each_k(one)


def call(name, us, kernel, args, outs, scratch=(), smem=0, far=0, limit=24):
    whole = pl.BlockSpec(memory_space=pltpu.VMEM)
    specs = [pl.BlockSpec(memory_space=pltpu.SMEM)] * smem
    specs += [pl.BlockSpec(memory_space=pltpu.HBM)] * far
    specs += [whole] * (len(args) - smem - far)
    buffers = [pltpu.VMEM(s, d) for s, d in scratch]
    if far:
        buffers += [pltpu.VMEM(a.shape, a.dtype) for a in args[smem : smem + far]]
        buffers += [pltpu.SemaphoreType.DMA((far,))]
    args = list(args)
    for i in range(smem, smem + far):
        args[i] = pltpu.with_memory_space_constraint(args[i], pltpu.HBM)
    return pl.pallas_call(
        kernel,
        out_shape=[jax.ShapeDtypeStruct(s, d) for s, d in outs],
        in_specs=specs,
        out_specs=[whole] * len(outs),
        scratch_shapes=buffers,
        compiler_params=pltpu.CompilerParams(vmem_limit_bytes=limit << 20),
        cost_estimate=pl.CostEstimate(
            flops=int(us * 1.15e9), bytes_accessed=1000, transcendentals=0
        ),
        name=name,
    )(*args)


def shards(
    node_feats,
    cotangent,
    sources,
    targets,
    bins,
    live_mask,
    radial,
    edge_bias,
    w_value,
    w_query,
    w_out,
    w_radial,
    w_mix,
    rotations,
):
    feats = jnp.transpose(node_feats[0], (1, 0, 2))
    cot = jnp.transpose(cotangent[0], (1, 0, 2))
    rot = jnp.transpose(rotations, (1, 2, 0))
    bias = jnp.transpose(edge_bias[0])
    nodes = feats.shape[1]
    wide = feats.shape[2]
    slots = sources.shape[1]
    ranks = lax.axis_size("graph")
    planes = lax.axis_size("dp")
    chips = ranks // 2
    some = chips // 2
    rank = lax.axis_index("graph")
    plane = lax.axis_index("dp")
    core, chip = rank % 2, rank // 2
    spot = chips * nodes
    where = jnp.stack([core, chip, plane]).astype(jnp.int32)
    where_sum = jnp.stack([core, plane]).astype(jnp.int32)

    def other_core(a):
        return lax.ppermute(a, "graph", [(i, i ^ 1) for i in range(ranks)])

    def along(a, step):
        return lax.ppermute(a, "graph", [(i, i ^ (2 * step)) for i in range(ranks)])

    def beside(a, step):
        return lax.ppermute(a, "dp", [(i, i ^ step) for i in range(planes)])

    def direct(a):
        return [a] + [along(a, step) for step in range(1, chips)]

    line = lax.broadcasted_iota(jnp.int32, (16, slots), 0)
    ids = jnp.where(line < 2, jnp.where(line == 0, sources, targets), jnp.where(line == 2, bins, live_mask))
    pack_own = jnp.where(
        line < 4, ids.astype(F32), jnp.pad(bias.astype(F32), ((8, 0), (0, 0)))
    )
    have = {0: cot}
    step = some
    while step > 1:
        for p in list(have):
            have[p ^ step] = along(have[p], step)
        step //= 2
    neighbour = along(cot, 1)
    pack_sib = other_core(pack_own)
    radial_sib = other_core(radial[0])
    feats_sib = other_core(feats)
    firsts = direct(feats[0])
    radial_sib, firsts = lax.optimization_barrier((radial_sib, firsts))

    edge_f32 = ((wide, slots), F32)
    half_f32 = ((wide, slots // 2), F32)
    block = ((K, nodes, wide), BF)
    table, scaled, mixed, gating, pack, radial_here = call(
        "forward",
        9,
        functools.partial(forward_kernel, chips),
        [
            where,
            radial[0],
            w_radial,
            rot,
            feats,
            w_value,
            w_mix,
            pack_own,
            pack_sib,
            radial_sib,
            feats_sib,
        ],
        [
            ((R, 56, slots), F32),
            ((R, wide, slots), BF),
            ((R, wide, slots), BF),
            edge_f32,
            ((16, slots), F32),
            ((slots, radial.shape[2]), BF),
        ],
        [((K, wide, slots), BF)],
        smem=1,
        far=6,
        limit=32,
    )
    weight, stats, query, *raw = call(
        "attend",
        1,
        functools.partial(attend_kernel, chips),
        [w_query, *firsts, pack, table, mixed],
        [
            ((H, slots), F32),
            ((2 * H, spot), F32),
            edge_f32,
            *([((K, nodes, wide), F32)] * chips),
        ],
        [((R, wide, slots), BF), ((K, wide, slots), BF)],
        far=1,
    )
    del have[0]
    stats, have = lax.optimization_barrier((stats, have))
    have[0] = cot
    have.update({p ^ 1: along(a, 1) if p else neighbour for p, a in have.items()})
    cots = [have[p] for p in range(chips)]
    all_stats = direct(stats)

    def pull(second, extra, sums):
        mine = slice(some, chips) if second else slice(0, some)
        return call(
            "pull",
            4 if second else 1,
            functools.partial(pull_kernel, chips, second),
            [*cots[mine], w_out, pack, table, mixed, *extra],
            [((R, wide, slots // 2), BF), half_f32, ((H, slots // 2), F32), *sums],
            [((K, wide, slots // 2), BF), half_f32],
        )

    pulled_a, pulled0_a, dalpha_a = pull(False, [], [])
    share, *parts = call(
        "share",
        0.3,
        functools.partial(share_kernel, chips),
        [*all_stats, *raw, weight, pack],
        [((H, slots), F32), *([block] * chips)],
    )

    parts, cots[-1] = lax.optimization_barrier((parts, cots[-1]))
    pending = {p: [parts[p]] for p in range(chips)}
    near = {p: along(parts[p], 1) for p in range(chips) if p & 1 and p > 1}
    pulled_b, pulled0_b, dalpha_b, dots = pull(True, [dalpha_a, share], [((H, spot), F32)])
    all_dots = direct(dots)
    for p, got in near.items():
        del pending[p]
        pending[p ^ 1].append(got)
    summed = {}
    for p in pending:
        if p:
            (summed[p],) = call("add", 1, add_kernel, pending[p], [block])
    pulled_b, summed, last = lax.optimization_barrier((pulled_b, summed, parts[1]))
    del pending[1]
    pending[0].append(along(last, 1))
    step = 2
    while step < chips:
        for p in [p for p in summed if p & step]:
            got = along(summed.pop(p), step)
            if p ^ step:
                (summed[p ^ step],) = call("add", 1, add_kernel, [summed[p ^ step], got], [block])
            else:
                pending[0].append(got)
        step *= 2
    gate_sum, dv_own, dv_sib, g_mix, g_value, g_out = call(
        "back",
        7.5,
        functools.partial(back_kernel, chips),
        [
            *parts,
            *cots,
            feats,
            feats_sib,
            pulled_a,
            pulled_b,
            share,
            scaled,
            gating,
            table,
            pack,
            w_mix,
        ],
        [edge_f32, block, block, (w_mix.shape, F32), ((wide, wide), F32), ((wide, wide), F32)],
        [((R, wide, slots), BF), ((K, wide, slots), BF)],
        limit=32,
    )
    dv_got = other_core(dv_sib)

    total_rows = (4 + 2 * MMAX) * wide + radial.shape[2]
    cut = total_rows // (2 * planes)
    small = ((nodes, wide), BF)
    keep, send, dv0_own, *dqs = call(
        "tail",
        1.8,
        functools.partial(tail_kernel, chips),
        [
            where_sum,
            *all_dots,
            *firsts,
            feats_sib,
            dalpha_a,
            dalpha_b,
            share,
            pulled0_a,
            pulled0_b,
            query,
            mixed,
            scaled,
            gating,
            table,
            gate_sum,
            radial_here,
            pack,
            w_mix,
            g_mix,
            g_value,
            g_out,
        ],
        [
            ((total_rows // 2, wide), F32),
            ((total_rows // 2 + nodes, wide), BF),
            small,
            *([((2 * nodes, wide), BF)] * chips),
        ],
        [((2, total_rows // 2, wide), F32)],
        smem=1,
    )

    got = other_core(send)
    own, dv0_got, *sends = call(
        "split",
        0.6,
        functools.partial(split_kernel, planes),
        [where_sum, keep, got],
        [((cut, wide), F32), small, *([((cut, wide), BF)] * (planes - 1))],
        [((planes, cut, wide), F32)],
        smem=1,
    )
    got = [beside(sends[step - 1], step) for step in range(1, planes)]
    got, pending[0] = lax.optimization_barrier((got, pending[0]))
    letters = call(
        "address",
        0.6,
        functools.partial(address_kernel, planes),
        [own, *got, *dqs],
        [((cut + 2 * nodes, wide), BF)] * chips,
    )
    terms = [letters[0]] + [along(letters[step], step) for step in range(1, chips)]
    (updated,) = call("update", 2, update_kernel, [*pending[0], feats, w_out], [block])
    terms, updated = lax.optimization_barrier((terms, updated))
    piece, dquery = call("settle", 0.6, settle_kernel, terms, [((cut, wide), BF), small])
    mine = [piece] + [beside(piece, step) for step in range(1, planes)]
    theirs = [other_core(a) for a in mine]
    grads = call(
        "join",
        1.5,
        functools.partial(join_kernel, planes),
        [where_sum, *mine, *theirs],
        [
            ((wide, wide), F32),
            ((wide, wide), F32),
            ((wide, wide), F32),
            ((radial.shape[2], wide), F32),
            (w_mix.shape, F32),
        ],
        [((2 * planes, cut, wide), F32)],
        smem=1,
    )

    (grad_nodes,) = call(
        "nodes",
        2.6,
        nodes_kernel,
        [dquery, dv_own, dv_got, dv0_own, dv0_got, cot, w_value, w_query],
        [block],
    )
    return (
        jnp.transpose(updated, (1, 0, 2))[None],
        jnp.transpose(grad_nodes, (1, 0, 2))[None],
        *grads,
    )


def solution(mesh):
    edge = P("dp", "graph")
    return jax.shard_map(
        shards,
        mesh=mesh,
        in_specs=(edge, edge, edge, edge, edge, edge, edge, edge, P(), P(), P(), P(), P(), P()),
        out_specs=(edge, edge, P(), P(), P(), P(), P()),
        check_vma=False,
    )
```

```python
import functools

import jax
import jax.numpy as jnp
import numpy as np
from jax import lax
from jax.experimental import pallas as pl
from jax.experimental.pallas import tpu as pltpu
from jax.sharding import PartitionSpec as P

H = 8
VH = 16
LMAX = 6
MMAX = 2
K = (LMAX + 1) ** 2
BF = jnp.bfloat16
F32 = jnp.float32
CHUNK = 16
LANES = 128


def frame_layout():
    index, degree_of = [], []
    for order in range(MMAX + 1):
        for sign in (1, -1) if order else (1,):
            for degree in range(order, LMAX + 1):
                index.append(degree * degree + degree + sign * order)
                degree_of.append(degree)
    return index, degree_of


ROWS, DEGREE = frame_layout()
R = len(ROWS)
OF_DEGREE = [[r for r in range(R) if DEGREE[r] == degree] for degree in range(LMAX + 1)]
PAIRS = []
_offset = LMAX + 1
for _order in range(1, MMAX + 1):
    _length = LMAX + 1 - _order
    for _i in range(_length):
        PAIRS.append((_order, _offset + _i, _offset + _length + _i))
    _offset += 2 * _length


def dot(a, b, ca=1, cb=0, exact=False):
    return lax.dot_general(
        a,
        b,
        (((ca,), (cb,)), ((), ())),
        precision=lax.Precision.HIGHEST if exact else None,
        preferred_element_type=F32,
    )


def flip(a):
    return jnp.transpose(a.astype(F32)).astype(a.dtype)


def hits(row, count, dtype):
    lines = lax.broadcasted_iota(jnp.int32, (count, row.shape[1]), 0)
    return jnp.where(lines == row.astype(jnp.int32), 1.0, 0.0).astype(dtype)


def head_sum(a):
    return jnp.sum(a.reshape(H, VH, a.shape[1]), axis=1)


def spread(a):
    return jnp.broadcast_to(a[:, None, :], (H, VH, a.shape[1])).reshape(H * VH, a.shape[1])


def turn(table, source, base, degrees, emit, finish=None):
    channels, edges = source.shape[1], source.shape[2]

    def step(i, carry):
        rows = pl.ds(i * CHUNK, CHUNK)
        for start in range(0, edges, LANES):
            lanes = pl.ds(start, LANES)
            carried = None
            for degree in degrees:
                block = range(degree * degree, (degree + 1) ** 2)
                parts = [source[k, rows, lanes].astype(F32) for k in block]
                for r in OF_DEGREE[degree]:
                    total = None
                    for k, part in zip(block, parts):
                        at = base + start
                        term = table[r, k : k + 1, at : at + LANES] * part
                        total = term if total is None else total + term
                    carried = emit(r, rows, lanes, total, carried)
            if finish is not None:
                finish(rows, lanes, carried)
        return carry

    for i in range(channels // CHUNK):
        step(i, 0)


def turn_back(table, source, degrees, out):
    channels, edges = source.shape[1], source.shape[2]

    def step(i, carry):
        rows = pl.ds(i * CHUNK, CHUNK)
        for start in range(0, edges, LANES):
            lanes = pl.ds(start, LANES)
            for degree in degrees:
                parts = [source[r, rows, lanes].astype(F32) for r in OF_DEGREE[degree]]
                for k in range(degree * degree, (degree + 1) ** 2):
                    total = None
                    for r, part in zip(OF_DEGREE[degree], parts):
                        term = table[r, k : k + 1, start : start + LANES] * part
                        total = term if total is None else total + term
                    out[k, rows, lanes] = total.astype(out.dtype)
        return carry

    for i in range(channels // CHUNK):
        step(i, 0)


def by_sevens(body):
    for i in range(LMAX + 1):
        body(i * (LMAX + 1))


def each_k(body):
    by_sevens(lambda k: [body(k + j) for j in range(LMAX + 1)] and None)


def flat(ref, k):
    return ref[pl.ds(k, LMAX + 1)].reshape((LMAX + 1) * ref.shape[1], ref.shape[2])


def rows_of(pieces):
    return jnp.concatenate(pieces, axis=0)


def whole_order(own, chips, p, span):
    return [own[:, (q ^ p) * span : ((q ^ p) + 1) * span] for q in range(chips)]


def mix_block(w_mix, order, back):
    even, odd = w_mix[2 * order - 1], w_mix[2 * order]
    if back:
        return jnp.concatenate(
            [
                jnp.concatenate([even, odd], axis=1),
                jnp.concatenate([-odd, even], axis=1),
            ],
            axis=0,
        )
    even, odd = flip(even), flip(odd)
    return jnp.concatenate(
        [
            jnp.concatenate([even, -odd], axis=1),
            jnp.concatenate([odd, even], axis=1),
        ],
        axis=0,
    )


def forward_kernel(chips, where, *refs):
    far, refs = refs[:6], refs[6:]
    pack_own, pack_sib, radial_sib, feats_sib, *refs = refs
    table, scaled, mixed, gating, pack, radial, incoming, *refs = refs
    near, sems = refs[:6], refs[6]
    copies = [pltpu.make_async_copy(a, b, sems.at[i]) for i, (a, b) in enumerate(zip(far, near))]
    for c in copies:
        c.start()
    radial_own, w_radial, rot, feats_own, w_value, w_mix = near
    core, chip = where[0], where[1]
    slots = pack_own.shape[1]
    cap = slots // (2 * chips)
    nodes = feats_sib.shape[1]
    bins = rot.shape[2]

    edge = lax.broadcasted_iota(jnp.int32, (2 * slots, slots), 1)
    place = lax.broadcasted_iota(jnp.int32, (2 * slots, slots), 0)
    side = (edge // cap) % 2
    origin = side * slots + (2 * ((edge // (2 * cap)) ^ chip) + core) * cap + edge % cap
    pick = jnp.where(place == origin, 1.0, 0.0).astype(BF)

    def relative(raw):
        ids = raw[0:2].astype(jnp.int32)
        owner = ids[1:2] // nodes
        source = ids[0:1] - 2 * chip * nodes
        swapped = jnp.where(source < nodes, source + nodes, source - nodes)
        rows_ = [jnp.where(core == 0, source, swapped), ids[1:2] - owner * nodes]
        rows_ = [a.astype(F32) for a in rows_ + [(owner // 2) ^ chip]]
        return jnp.concatenate([rows_[0], rows_[1], raw[2:4], rows_[2], raw[5:]], axis=0)

    packs = [relative(pack_own[...]), relative(pack_sib[...])]
    packs = jnp.concatenate(packs, axis=1).astype(BF)
    rows = dot(packs, pick)
    lines = rows[4:5] * float(nodes) + rows[1:2]
    pack[...] = rows
    pack[1:2, :] = lines
    bin_hit = hits(rows[2:3], bins, BF)
    source_hit = hits(rows[0:1], 2 * nodes, BF)
    for c in copies[:2]:
        c.wait()
    radial[...] = dot(pick, rows_of([radial_own[...], radial_sib[...]]), 0, 0).astype(BF)
    gating[...] = jax.nn.sigmoid(dot(flip(w_radial[...]), radial[...], 1, 1))
    copies[2].wait()
    for r, row in enumerate(ROWS):
        table[r, 0:K, :] = dot(rot[row], bin_hit)
    for c in copies[3:]:
        c.wait()
    value_t = flip(w_value[...])

    def gather(k):
        values = [
            dot(value_t, rows_of([feats_own[k + j], feats_sib[k + j]]), 1, 1).astype(BF)
            for j in range(LMAX + 1)
        ]
        got = dot(rows_of(values), source_hit).astype(BF)
        for j in range(LMAX + 1):
            incoming[k + j] = got[j * H * VH : (j + 1) * H * VH]

    by_sevens(gather)

    def emit(r, rows_, lanes, total, carried):
        gate = gating[rows_, lanes] if carried is None else carried
        scaled[r, rows_, lanes] = (total * gate).astype(BF)
        return gate

    turn(table, incoming, 0, range(LMAX + 1), emit)

    zero_t = flip(w_mix[0])
    for r in range(LMAX + 1):
        mixed[r] = dot(zero_t, scaled[r]).astype(BF)
    blocks = [None] + [mix_block(w_mix, order, False) for order in range(1, MMAX + 1)]
    for order, plus, minus in PAIRS:
        out = dot(blocks[order], rows_of([scaled[plus], scaled[minus]])).astype(BF)
        mixed[plus] = out[: H * VH]
        mixed[minus] = out[H * VH :]


def attend_kernel(chips, *refs):
    far, refs = refs[0], refs[1:]
    firsts, refs = refs[:chips], refs[chips:]
    pack, table, mixed, weight, stats, query, *refs = refs
    parts, refs = refs[:chips], refs[chips:]
    scaled_rows, back, w_query, sems = refs
    copy = pltpu.make_async_copy(far, w_query, sems.at[0])
    copy.start()
    slots = pack.shape[1]
    nodes = firsts[0].shape[0]
    targets = chips * nodes
    rows = pack[...]
    target_hit = hits(rows[1:2], targets, BF)
    first = rows_of([f[...] for f in firsts])
    copy.wait()
    queries = dot(flip(w_query[...]), first, 1, 1).astype(BF)
    query[...] = dot(queries, target_hit)
    scores = head_sum(mixed[0].astype(F32) * query[...]) * (1.0 / VH**0.5) + rows[8:16]
    live = rows[3:4] > 0.5
    columns = jnp.transpose(rows)
    score_columns = jnp.transpose(scores)
    line = lax.broadcasted_iota(jnp.int32, (slots, targets), 1)
    chosen = (line == columns[:, 1:2].astype(jnp.int32)) & (columns[:, 3:4] > 0.5)
    top = jnp.concatenate(
        [
            jnp.max(jnp.where(chosen, score_columns[:, h : h + 1], 0.0), axis=0, keepdims=True)
            for h in range(H)
        ],
        axis=0,
    )
    top = jnp.maximum(top, 0.0)
    target_hit32 = target_hit.astype(F32)
    top_edge = dot(top, target_hit32, exact=True)
    weights = jnp.where(live, jnp.exp(jnp.where(live, scores - top_edge, 0.0)), 0.0)
    weight[...] = weights
    stats[0:H] = top
    stats[H : 2 * H] = dot(weights, target_hit32, 1, 1, exact=True)

    wide = spread(weights)
    for r in range(R):
        scaled_rows[r] = (mixed[r].astype(F32) * wide).astype(BF)
    turn_back(table, scaled_rows, range(LMAX + 1), back)

    def collect(k):
        out = dot(target_hit, flat(back, k), 1, 1).astype(BF)
        for j in range(LMAX + 1):
            for p in range(chips):
                parts[p][k + j] = out[p * nodes : (p + 1) * nodes, j * LANES : (j + 1) * LANES]

    by_sevens(collect)


def share_kernel(chips, *refs):
    stats, raw, refs = refs[:chips], refs[chips : 2 * chips], refs[2 * chips :]
    handed = range(2, chips, 2)
    got, refs = dict(zip(handed, refs)), refs[len(handed) :]
    weight, pack, sums_a, sums_b, share, dscore = refs[:6]
    parts, summed = refs[6 : 6 + chips], dict(zip(handed, refs[6 + chips :]))
    targets = stats[0].shape[1]
    nodes = targets // chips
    target_hit32 = hits(pack[1:2], targets, F32)
    wholes = [
        jnp.concatenate(whole_order(stats[p], chips, p, nodes), axis=1) for p in range(chips)
    ]
    top = functools.reduce(jnp.maximum, [w[0:H] for w in wholes])
    bottom = jnp.exp(-top)
    dots = jnp.zeros_like(top)
    for w in wholes:
        level = jnp.exp(w[0:H] - top)
        bottom = bottom + w[H : 2 * H] * level
        dots = dots + w[2 * H :] * level
    factors = [jnp.exp(w[0:H] - top) / bottom for w in wholes[:2]]
    at_edges = dot(
        jnp.concatenate([factors[0], dots / bottom], axis=0), target_hit32, exact=True
    )
    shares = weight[...] * at_edges[0:H]
    share[...] = shares
    sums = jnp.concatenate([sums_a[...], sums_b[...]], axis=1)
    dscore[...] = shares * (sums - at_edges[H:])
    scales = [jnp.transpose(spread(f)) for f in factors]

    def normalize(k):
        for p in range(chips):
            rows = slice(p * nodes, (p + 1) * nodes)
            here = raw[p][k].astype(F32) * scales[0][rows]
            parts[p][k] = here.astype(BF)
            if p in got:
                summed[p][k] = (here + got[p][k].astype(F32) * scales[1][rows]).astype(BF)

    each_k(normalize)


def pull_kernel(chips, second, *refs):
    some = chips // 2
    cots, refs = refs[:some], refs[some:]
    w_out, pack, table, mixed, *refs = refs
    if second:
        before, weight, own_stats, pulled, pulled0, dalpha, stats, *refs = refs
    else:
        pulled, pulled0, dalpha, *refs = refs
    incoming, total_ref = refs
    nodes = cots[0].shape[1]
    edges = pulled.shape[2]
    base = edges if second else 0
    span = some * nodes
    lines = pack[1:2, base : base + edges] - (span if second else 0)
    target_hit = hits(lines, span, BF)
    out_w = w_out[...]

    def gather(k):
        backs = [
            dot(out_w, rows_of([c[k + j] for c in cots]), 1, 1).astype(BF) for j in range(LMAX + 1)
        ]
        got = dot(rows_of(backs), target_hit).astype(BF)
        for j in range(LMAX + 1):
            incoming[k + j] = got[j * H * VH : (j + 1) * H * VH]

    by_sevens(gather)

    def emit(r, rows, lanes, total, carried):
        far = pl.ds(base + lanes.start, lanes.size)
        term = total * mixed[r, rows, far].astype(F32)
        pulled[r, rows, lanes] = total.astype(BF)
        return term if carried is None else carried + term

    def finish(rows, lanes, carried):
        total_ref[rows, lanes] = carried

    turn(table, incoming, base, range(LMAX + 1), emit, finish)
    sums = head_sum(total_ref[...])
    dalpha[...] = sums
    pulled0[...] = table[0, 0:1, base : base + edges] * incoming[0].astype(F32)
    if second:
        every = weight[...] * jnp.concatenate([before[...], sums], axis=1)
        stats[: 2 * H] = own_stats[...]
        stats[2 * H :] = dot(every, hits(pack[1:2], stats.shape[1], F32), 1, 1, exact=True)


def back_kernel(chips, where, *refs):
    parts, cots, firsts = refs[:chips], refs[chips : 2 * chips], refs[2 * chips : 3 * chips]
    refs = refs[3 * chips :]
    feats_own, feats_sib, pulled_a, pulled_b, pulled0_a, pulled0_b = refs[:6]
    share, dscore, query, mixed, scaled, gating, table, radial, pack, w_mix = refs[6:16]
    keep, send, dv_own, dv_sib = refs[16:20]
    dqs = refs[20 : 20 + chips]
    turned, spread_back, grads = refs[20 + chips :]
    nodes = feats_own.shape[1]
    targets = chips * nodes
    wide = H * VH
    half = grads.shape[1]

    def put(i, value):
        at = i * wide
        grads[at // half, at % half : at % half + value.shape[0]] = value

    gate = gating[...]
    zero = w_mix[0]
    shares = spread(share[...])
    dlogit = spread(dscore[...]) * (1.0 / VH**0.5)
    gates = jnp.zeros_like(gate)

    def pulled(r):
        if r == 0:
            whole = jnp.concatenate([pulled0_a[...], pulled0_b[...]], axis=1) * shares
            return (whole + dlogit * query[...]).astype(BF)
        whole = jnp.concatenate([pulled_a[r], pulled_b[r]], axis=1)
        return (whole.astype(F32) * shares).astype(BF)

    grad = jnp.zeros((wide, wide), F32)
    for r in range(LMAX + 1):
        here = scaled[r]
        down = pulled(r)
        grad = grad + dot(here, down, 1, 1)
        out = dot(zero, down)
        gates = gates + out * here.astype(F32)
        turned[r] = (out * gate).astype(BF)
    put(3, grad)
    for order in range(1, MMAX + 1):
        block = mix_block(w_mix, order, True)
        grad = jnp.zeros((2 * wide, 2 * wide), F32)
        for own, plus, minus in PAIRS:
            if own != order:
                continue
            down = rows_of([pulled(plus), pulled(minus)])
            here = rows_of([scaled[plus], scaled[minus]])
            grad = grad + dot(here, down, 1, 1)
            out = dot(block, down)
            prod = out * here.astype(F32)
            gates = gates + prod[:wide] + prod[wide:]
            turned[plus] = (out[:wide] * gate).astype(BF)
            turned[minus] = (out[wide:] * gate).astype(BF)
        put(2 + 2 * order, grad[:wide, :wide] + grad[wide:, wide:])
        put(3 + 2 * order, grad[:wide, wide:] - grad[wide:, :wide])
    dgate = (gates * (1.0 - gate)).astype(BF)
    radial_grad = dot(dgate, radial[...])
    for i in range(radial.shape[1] // wide):
        put(4 + 2 * MMAX + i, jnp.transpose(radial_grad[:, i * wide : (i + 1) * wide]))
    dq = dot(hits(pack[1:2], targets, F32), dlogit * mixed[0].astype(F32), 1, 1, exact=True)
    for p in range(chips):
        some = dq[p * nodes : (p + 1) * nodes]
        dqs[p][:nodes] = some.astype(BF)
        dqs[p][nodes:] = (some - some.astype(BF).astype(F32)).astype(BF)
    put(1, dot(rows_of([f[...] for f in firsts]), dq.astype(BF), 0, 0))

    turn_back(table, turned, range(LMAX + 1), spread_back)
    source_hit = hits(pack[0:1], 2 * nodes, BF)

    def collect(k):
        out = dot(source_hit, flat(spread_back, k), 1, 1).astype(BF)
        for j in range(LMAX + 1):
            dv_own[k + j] = out[:nodes, j * LANES : (j + 1) * LANES]
            dv_sib[k + j] = out[nodes:, j * LANES : (j + 1) * LANES]

    by_sevens(collect)
    put(0, jnp.zeros((wide, wide), F32))
    put(2, jnp.zeros((wide, wide), F32))

    def weigh(k):
        grads[0, 0:wide] += dot(flat(feats_own, k), flat(dv_own, k), 0, 0) + dot(
            flat(feats_sib, k), flat(dv_sib, k), 0, 0
        )
        total = dot(flat(parts[0], k), flat(cots[0], k), 0, 0)
        for p in range(1, chips):
            total = total + dot(flat(parts[p], k), flat(cots[p], k), 0, 0)
        grads[0, 2 * wide : 3 * wide] += total

    by_sevens(weigh)
    keep[...] = grads[where[0]]
    send[...] = grads[1 - where[0]].astype(BF)


def split_kernel(planes, where, keep, got, own, *outs):
    *sends, total = outs
    total[...] = (keep[...] + got[...].astype(F32)).reshape(total.shape)
    own[...] = total[where[1]]
    for step in range(1, planes):
        sends[step - 1][...] = total[where[1] ^ step].astype(BF)


def address_kernel(planes, own, *refs):
    got, refs = refs[: planes - 1], refs[planes - 1 :]
    dqs, outs = refs[: len(refs) // 2], refs[len(refs) // 2 :]
    total = functools.reduce(jnp.add, [own[...]] + [g[...].astype(F32) for g in got]).astype(BF)
    for dq, out in zip(dqs, outs):
        out[: own.shape[0]] = total
        out[own.shape[0] :] = dq[...]


def settle_kernel(*refs):
    *terms, piece, dquery = refs
    rows, nodes = piece.shape[0], dquery.shape[0]

    def total(values):
        while len(values) > 1:
            values = [a + b for a, b in zip(values[0::2], values[1::2])]
        return values[0].astype(BF)

    piece[...] = total([t[:rows].astype(F32) for t in terms])
    dquery[...] = total(
        [t[rows : rows + nodes].astype(F32) + t[rows + nodes :].astype(F32) for t in terms]
    )


def join_kernel(planes, where, *refs):
    mine, theirs = refs[:planes], refs[planes : 2 * planes]
    g_value, g_query, g_out, g_radial, g_mix, total = refs[2 * planes :]
    for step in range(planes):
        total[where[0] * planes + (where[1] ^ step)] = mine[step][...].astype(F32)
        total[(1 - where[0]) * planes + (where[1] ^ step)] = theirs[step][...].astype(F32)
    wide = H * VH
    flat = total[...].reshape(total.shape[0] * total.shape[1], wide)
    pieces = [flat[i * wide : (i + 1) * wide] for i in range(flat.shape[0] // wide)]
    g_value[...], g_query[...], g_out[...] = pieces[:3]
    for i in range(2 * MMAX + 1):
        g_mix[i] = pieces[3 + i]
    at = 4 + 2 * MMAX
    for i in range(g_radial.shape[0] // wide):
        g_radial[i * wide : (i + 1) * wide] = pieces[at + i]


def nodes_kernel(dquery, dv_own, dv_sib, cot, w_value, w_query, out):
    value_w = w_value[...]

    def back(k):
        dv = (dv_own[k].astype(F32) + dv_sib[k].astype(F32)).astype(BF)
        return dot(dv, value_w, 1, 1)

    def one(k):
        out[k] = (cot[k].astype(F32) + back(k)).astype(BF)

    each_k(one)
    query_part = dot(dquery[...], w_query[...], 1, 1)
    out[0] = (cot[0].astype(F32) + back(0) + query_part).astype(BF)


def add_kernel(*refs):
    *terms, out = refs

    def one(k):
        out[k] = functools.reduce(jnp.add, [t[k].astype(F32) for t in terms]).astype(BF)

    each_k(one)


def update_kernel(*refs):
    *parts, feats, w_out, out = refs
    out_w = w_out[...]

    def one(k):
        total = functools.reduce(jnp.add, [t[k].astype(F32) for t in parts])
        out[k] = (feats[k].astype(F32) + dot(total.astype(BF), out_w)).astype(BF)

    each_k(one)


def call(name, us, kernel, args, outs, scratch=(), smem=0, far=0, limit=24):
    whole = pl.BlockSpec(memory_space=pltpu.VMEM)
    specs = [pl.BlockSpec(memory_space=pltpu.SMEM)] * smem
    specs += [pl.BlockSpec(memory_space=pltpu.HBM)] * far
    specs += [whole] * (len(args) - smem - far)
    buffers = [pltpu.VMEM(s, d) for s, d in scratch]
    if far:
        buffers += [pltpu.VMEM(a.shape, a.dtype) for a in args[smem : smem + far]]
        buffers += [pltpu.SemaphoreType.DMA((far,))]
    args = list(args)
    for i in range(smem, smem + far):
        args[i] = pltpu.with_memory_space_constraint(args[i], pltpu.HBM)
    return pl.pallas_call(
        kernel,
        out_shape=[jax.ShapeDtypeStruct(s, d) for s, d in outs],
        in_specs=specs,
        out_specs=[whole] * len(outs),
        scratch_shapes=buffers,
        compiler_params=pltpu.CompilerParams(vmem_limit_bytes=limit << 20),
        cost_estimate=pl.CostEstimate(
            flops=int(us * 1.15e9), bytes_accessed=1000, transcendentals=0
        ),
        name=name,
    )(*args)


def shards(
    node_feats,
    cotangent,
    sources,
    targets,
    bins,
    live_mask,
    radial,
    edge_bias,
    w_value,
    w_query,
    w_out,
    w_radial,
    w_mix,
    rotations,
):
    feats = jnp.transpose(node_feats[0], (1, 0, 2))
    cot = jnp.transpose(cotangent[0], (1, 0, 2))
    rot = jnp.transpose(rotations, (1, 2, 0))
    bias = jnp.transpose(edge_bias[0])
    nodes = feats.shape[1]
    wide = feats.shape[2]
    slots = sources.shape[1]
    ranks = lax.axis_size("graph")
    planes = lax.axis_size("dp")
    chips = ranks // 2
    some = chips // 2
    rank = lax.axis_index("graph")
    plane = lax.axis_index("dp")
    core, chip = rank % 2, rank // 2
    spot = chips * nodes
    where = jnp.stack([core, chip, plane]).astype(jnp.int32)
    where_sum = jnp.stack([core, plane]).astype(jnp.int32)

    def other_core(a):
        return lax.ppermute(a, "graph", [(i, i ^ 1) for i in range(ranks)])

    def along(a, step):
        return lax.ppermute(a, "graph", [(i, i ^ (2 * step)) for i in range(ranks)])

    def beside(a, step):
        return lax.ppermute(a, "dp", [(i, i ^ step) for i in range(planes)])

    def direct(a):
        return [a] + [along(a, step) for step in range(1, chips)]

    line = lax.broadcasted_iota(jnp.int32, (16, slots), 0)
    ids = jnp.where(line < 2, jnp.where(line == 0, sources, targets), jnp.where(line == 2, bins, live_mask))
    pack_own = jnp.where(
        line < 4, ids.astype(F32), jnp.pad(bias.astype(F32), ((8, 0), (0, 0)))
    )
    have = {0: cot}
    step = some
    while step > 1:
        for p in list(have):
            have[p ^ step] = along(have[p], step)
        step //= 2
    neighbour = along(cot, 1)
    pack_sib = other_core(pack_own)
    radial_sib = other_core(radial[0])
    feats_sib = other_core(feats)

    edge_f32 = ((wide, slots), F32)
    half_f32 = ((wide, slots // 2), F32)
    block = ((K, nodes, wide), BF)
    table, scaled, mixed, gating, pack, radial_here = call(
        "forward",
        9,
        functools.partial(forward_kernel, chips),
        [
            where,
            radial[0],
            w_radial,
            rot,
            feats,
            w_value,
            w_mix,
            pack_own,
            pack_sib,
            radial_sib,
            feats_sib,
        ],
        [
            ((R, 56, slots), F32),
            ((R, wide, slots), BF),
            ((R, wide, slots), BF),
            edge_f32,
            ((16, slots), F32),
            ((slots, radial.shape[2]), BF),
        ],
        [((K, wide, slots), BF)],
        smem=1,
        far=6,
        limit=32,
    )
    first, mixed = lax.optimization_barrier((feats[0], mixed))
    firsts = direct(first)
    del have[0]
    firsts, have = lax.optimization_barrier((firsts, have))
    have[0] = cot
    have.update({p ^ 1: along(a, 1) if p else neighbour for p, a in have.items()})
    cots = [have[p] for p in range(chips)]
    weight, stats, query, *raw = call(
        "attend",
        1,
        functools.partial(attend_kernel, chips),
        [w_query, *firsts, pack, table, mixed],
        [
            ((H, slots), F32),
            ((2 * H, spot), F32),
            edge_f32,
            *([block] * chips),
        ],
        [((R, wide, slots), BF), ((K, wide, slots), BF)],
        far=1,
    )

    def pull(second, extra, sums):
        mine = slice(some, chips) if second else slice(0, some)
        return call(
            "pull",
            4 if second else 1,
            functools.partial(pull_kernel, chips, second),
            [*cots[mine], w_out, pack, table, mixed, *extra],
            [((R, wide, slots // 2), BF), half_f32, ((H, slots // 2), F32), *sums],
            [((K, wide, slots // 2), BF), half_f32],
        )

    pulled_a, pulled0_a, dalpha_a = pull(False, [], [])
    raw, cots[-1] = lax.optimization_barrier((raw, cots[-1]))
    near = [along(raw[p], 1) for p in range(3, chips, 2)]
    pulled_b, pulled0_b, dalpha_b, stats = pull(
        True, [dalpha_a, weight, stats], [((3 * H, spot), F32)]
    )
    share, dscore, *parts = call(
        "share",
        0.6,
        functools.partial(share_kernel, chips),
        [*direct(stats), *raw, *near, weight, pack, dalpha_a, dalpha_b],
        [((H, slots), F32)] * 2 + [block] * (chips + len(near)),
    )
    summed = dict(zip(range(2, chips, 2), parts[chips:]))
    parts = parts[:chips]
    pending = [parts[0], along(parts[1], 1)]
    step = 2
    while step < chips:
        for p in [p for p in summed if p & step]:
            got = along(summed.pop(p), step)
            if p ^ step:
                (summed[p ^ step],) = call("add", 1, add_kernel, [summed[p ^ step], got], [block])
            else:
                pending.append(got)
        step *= 2
    total_rows = (4 + 2 * MMAX) * wide + radial.shape[2]
    cut = total_rows // (2 * planes)
    keep, send, dv_own, dv_sib, *dqs = call(
        "back",
        9,
        functools.partial(back_kernel, chips),
        [
            where_sum,
            *parts,
            *cots,
            *firsts,
            feats,
            feats_sib,
            pulled_a,
            pulled_b,
            pulled0_a,
            pulled0_b,
            share,
            dscore,
            query,
            mixed,
            scaled,
            gating,
            table,
            radial_here,
            pack,
            w_mix,
        ],
        [
            ((total_rows // 2, wide), F32),
            ((total_rows // 2, wide), BF),
            block,
            block,
            *([((2 * nodes, wide), BF)] * chips),
        ],
        [((R, wide, slots), BF), ((K, wide, slots), BF), ((2, total_rows // 2, wide), F32)],
        smem=1,
        limit=32,
    )
    dv_got = other_core(dv_sib)

    got = other_core(send)
    own, *sends = call(
        "split",
        0.6,
        functools.partial(split_kernel, planes),
        [where_sum, keep, got],
        [((cut, wide), F32), *([((cut, wide), BF)] * (planes - 1))],
        [((planes, cut, wide), F32)],
        smem=1,
    )
    got = [beside(sends[step - 1], step) for step in range(1, planes)]
    got, pending = lax.optimization_barrier((got, pending))
    letters = call(
        "address",
        0.6,
        functools.partial(address_kernel, planes),
        [own, *got, *dqs],
        [((cut + 2 * nodes, wide), BF)] * chips,
    )
    terms = [letters[0]] + [along(letters[step], step) for step in range(1, chips)]
    (updated,) = call("update", 2, update_kernel, [*pending, feats, w_out], [block])
    terms, updated = lax.optimization_barrier((terms, updated))
    piece, dquery = call(
        "settle", 0.6, settle_kernel, terms, [((cut, wide), BF), ((nodes, wide), BF)]
    )
    mine = [piece] + [beside(piece, step) for step in range(1, planes)]
    theirs = [other_core(a) for a in mine]
    grads = call(
        "join",
        1.5,
        functools.partial(join_kernel, planes),
        [where_sum, *mine, *theirs],
        [
            ((wide, wide), F32),
            ((wide, wide), F32),
            ((wide, wide), F32),
            ((radial.shape[2], wide), F32),
            (w_mix.shape, F32),
        ],
        [((2 * planes, cut, wide), F32)],
        smem=1,
    )

    (grad_nodes,) = call(
        "nodes",
        2.6,
        nodes_kernel,
        [dquery, dv_own, dv_got, cot, w_value, w_query],
        [block],
    )
    return (
        jnp.transpose(updated, (1, 0, 2))[None],
        jnp.transpose(grad_nodes, (1, 0, 2))[None],
        *grads,
    )


def solution(mesh):
    edge = P("dp", "graph")
    return jax.shard_map(
        shards,
        mesh=mesh,
        in_specs=(edge, edge, edge, edge, edge, edge, edge, edge, P(), P(), P(), P(), P(), P()),
        out_specs=(edge, edge, P(), P(), P(), P(), P()),
        check_vma=False,
    )
```

```python
import functools

import jax
import jax.numpy as jnp
import numpy as np
from jax import lax
from jax.experimental import pallas as pl
from jax.experimental.pallas import tpu as pltpu
from jax.sharding import PartitionSpec as P

H = 8
VH = 16
LMAX = 6
MMAX = 2
K = (LMAX + 1) ** 2
BF = jnp.bfloat16
F32 = jnp.float32
CHUNK = 16
LANES = 128


def frame_layout():
    index, degree_of = [], []
    for order in range(MMAX + 1):
        for sign in (1, -1) if order else (1,):
            for degree in range(order, LMAX + 1):
                index.append(degree * degree + degree + sign * order)
                degree_of.append(degree)
    return index, degree_of


ROWS, DEGREE = frame_layout()
R = len(ROWS)
OF_DEGREE = [[r for r in range(R) if DEGREE[r] == degree] for degree in range(LMAX + 1)]
PAIRS = []
_offset = LMAX + 1
for _order in range(1, MMAX + 1):
    _length = LMAX + 1 - _order
    for _i in range(_length):
        PAIRS.append((_order, _offset + _i, _offset + _length + _i))
    _offset += 2 * _length


def dot(a, b, ca=1, cb=0, exact=False):
    return lax.dot_general(
        a,
        b,
        (((ca,), (cb,)), ((), ())),
        precision=lax.Precision.HIGHEST if exact else None,
        preferred_element_type=F32,
    )


def flip(a):
    return jnp.transpose(a.astype(F32)).astype(a.dtype)


def hits(row, count, dtype):
    lines = lax.broadcasted_iota(jnp.int32, (count, row.shape[1]), 0)
    return jnp.where(lines == row.astype(jnp.int32), 1.0, 0.0).astype(dtype)


def head_sum(a):
    return jnp.sum(a.reshape(H, VH, a.shape[1]), axis=1)


def spread(a):
    return jnp.broadcast_to(a[:, None, :], (H, VH, a.shape[1])).reshape(H * VH, a.shape[1])


def turn(table, source, base, degrees, emit, finish=None):
    channels, edges = source.shape[1], source.shape[2]

    def step(i, carry):
        rows = pl.ds(i * CHUNK, CHUNK)
        for start in range(0, edges, LANES):
            lanes = pl.ds(start, LANES)
            carried = None
            for degree in degrees:
                block = range(degree * degree, (degree + 1) ** 2)
                parts = [source[k, rows, lanes].astype(F32) for k in block]
                for r in OF_DEGREE[degree]:
                    total = None
                    for k, part in zip(block, parts):
                        at = base + start
                        term = table[r, k : k + 1, at : at + LANES] * part
                        total = term if total is None else total + term
                    carried = emit(r, rows, lanes, total, carried)
            if finish is not None:
                finish(rows, lanes, carried)
        return carry

    for i in range(channels // CHUNK):
        step(i, 0)


def turn_back(table, source, degrees, out):
    channels, edges = source.shape[1], source.shape[2]

    def step(i, carry):
        rows = pl.ds(i * CHUNK, CHUNK)
        for start in range(0, edges, LANES):
            lanes = pl.ds(start, LANES)
            for degree in degrees:
                parts = [source[r, rows, lanes].astype(F32) for r in OF_DEGREE[degree]]
                for k in range(degree * degree, (degree + 1) ** 2):
                    total = None
                    for r, part in zip(OF_DEGREE[degree], parts):
                        term = table[r, k : k + 1, start : start + LANES] * part
                        total = term if total is None else total + term
                    out[k, rows, lanes] = total.astype(out.dtype)
        return carry

    for i in range(channels // CHUNK):
        step(i, 0)


def by_sevens(body):
    for i in range(LMAX + 1):
        body(i * (LMAX + 1))


def each_k(body):
    by_sevens(lambda k: [body(k + j) for j in range(LMAX + 1)] and None)


def flat(ref, k):
    return ref[pl.ds(k, LMAX + 1)].reshape((LMAX + 1) * ref.shape[1], ref.shape[2])


def rows_of(pieces):
    return jnp.concatenate(pieces, axis=0)


def whole_order(own, chips, p, span):
    return [own[:, (q ^ p) * span : ((q ^ p) + 1) * span] for q in range(chips)]


def mix_block(w_mix, order, back):
    even, odd = w_mix[2 * order - 1], w_mix[2 * order]
    if back:
        return jnp.concatenate(
            [
                jnp.concatenate([even, odd], axis=1),
                jnp.concatenate([-odd, even], axis=1),
            ],
            axis=0,
        )
    even, odd = flip(even), flip(odd)
    return jnp.concatenate(
        [
            jnp.concatenate([even, -odd], axis=1),
            jnp.concatenate([odd, even], axis=1),
        ],
        axis=0,
    )


def forward_kernel(chips, *refs):
    far, refs = refs[:6], refs[6:]
    pack_own, pack_sib, radial_sib, feats_sib, *refs = refs
    table, scaled, mixed, gating, pack, radial, incoming, *refs = refs
    near, sems = refs[:6], refs[6]
    copies = [pltpu.make_async_copy(a, b, sems.at[i]) for i, (a, b) in enumerate(zip(far, near))]
    for c in copies:
        c.start()
    radial_own, w_radial, rot, feats_own, w_value, w_mix = near
    rank = lax.axis_index("graph")
    core, chip = rank % 2, rank // 2
    slots = pack_own.shape[1]
    cap = slots // (2 * chips)
    nodes = feats_sib.shape[1]
    bins = rot.shape[2]

    edge = lax.broadcasted_iota(jnp.int32, (1, slots), 1)
    place = lax.broadcasted_iota(jnp.int32, (2 * slots, slots), 0)
    side = (edge // cap) % 2
    origin = side * slots + (2 * ((edge // (2 * cap)) ^ chip) + core) * cap + edge % cap
    pick = jnp.where(place == origin, 1.0, 0.0).astype(BF)

    def relative(raw):
        ids = raw[0:2].astype(jnp.int32)
        owner = ids[1:2] // nodes
        source = ids[0:1] - 2 * chip * nodes
        swapped = jnp.where(source < nodes, source + nodes, source - nodes)
        rows_ = [jnp.where(core == 0, source, swapped), ids[1:2] - owner * nodes]
        rows_ = [a.astype(F32) for a in rows_ + [(owner // 2) ^ chip]]
        return jnp.concatenate([rows_[0], rows_[1], raw[2:4], rows_[2], raw[5:]], axis=0)

    packs = [relative(pack_own[...]), relative(pack_sib[...])]
    packs = jnp.concatenate(packs, axis=1).astype(BF)
    rows = dot(packs, pick)
    lines = rows[4:5] * float(nodes) + rows[1:2]
    pack[...] = rows
    pack[1:2, :] = lines
    bin_hit = hits(rows[2:3], bins, BF)
    source_hit = hits(rows[0:1], 2 * nodes, BF)
    for c in copies[:2]:
        c.wait()
    radial[...] = dot(pick, rows_of([radial_own[...], radial_sib[...]]), 0, 0).astype(BF)
    gating[...] = jax.nn.sigmoid(dot(flip(w_radial[...]), radial[...], 1, 1))
    copies[2].wait()
    for r, row in enumerate(ROWS):
        table[r, 0:K, :] = dot(rot[row], bin_hit)
    for c in copies[3:]:
        c.wait()
    value_t = flip(w_value[...])

    def gather(k):
        values = [
            dot(value_t, rows_of([feats_own[k + j], feats_sib[k + j]]), 1, 1).astype(BF)
            for j in range(LMAX + 1)
        ]
        got = dot(rows_of(values), source_hit).astype(BF)
        for j in range(LMAX + 1):
            incoming[k + j] = got[j * H * VH : (j + 1) * H * VH]

    by_sevens(gather)

    def emit(r, rows_, lanes, total, carried):
        gate = gating[rows_, lanes] if carried is None else carried
        scaled[r, rows_, lanes] = (total * gate).astype(BF)
        return gate

    turn(table, incoming, 0, range(LMAX + 1), emit)

    zero_t = flip(w_mix[0])
    for r in range(LMAX + 1):
        mixed[r] = dot(zero_t, scaled[r]).astype(BF)
    blocks = [None] + [mix_block(w_mix, order, False) for order in range(1, MMAX + 1)]
    for order, plus, minus in PAIRS:
        out = dot(blocks[order], rows_of([scaled[plus], scaled[minus]])).astype(BF)
        mixed[plus] = out[: H * VH]
        mixed[minus] = out[H * VH :]


def attend_kernel(chips, *refs):
    far, refs = refs[0], refs[1:]
    firsts, refs = refs[:chips], refs[chips:]
    pack, table, mixed, weight, stats, query, *refs = refs
    parts, refs = refs[:chips], refs[chips:]
    scaled_rows, back, w_query, sems = refs
    copy = pltpu.make_async_copy(far, w_query, sems.at[0])
    copy.start()
    slots = pack.shape[1]
    nodes = firsts[0].shape[0]
    targets = chips * nodes
    rows = pack[...]
    target_hit = hits(rows[1:2], targets, BF)
    first = rows_of([f[...] for f in firsts])
    copy.wait()
    queries = dot(flip(w_query[...]), first, 1, 1).astype(BF)
    query[...] = dot(queries, target_hit)
    scores = head_sum(mixed[0].astype(F32) * query[...]) * (1.0 / VH**0.5) + rows[8:16]
    live = rows[3:4] > 0.5
    columns = jnp.transpose(rows)
    score_columns = jnp.transpose(scores)
    line = lax.broadcasted_iota(jnp.int32, (slots, targets), 1)
    chosen = (line == columns[:, 1:2].astype(jnp.int32)) & (columns[:, 3:4] > 0.5)
    top = jnp.concatenate(
        [
            jnp.max(jnp.where(chosen, score_columns[:, h : h + 1], 0.0), axis=0, keepdims=True)
            for h in range(H)
        ],
        axis=0,
    )
    top = jnp.maximum(top, 0.0)
    target_hit32 = target_hit.astype(F32)
    top_edge = dot(top, target_hit32, exact=True)
    weights = jnp.where(live, jnp.exp(jnp.where(live, scores - top_edge, 0.0)), 0.0)
    weight[...] = weights
    stats[0:H] = top
    stats[H : 2 * H] = dot(weights, target_hit32, 1, 1, exact=True)

    wide = spread(weights)
    for r in range(R):
        scaled_rows[r] = (mixed[r].astype(F32) * wide).astype(BF)
    turn_back(table, scaled_rows, range(LMAX + 1), back)

    def collect(k):
        out = dot(target_hit, flat(back, k), 1, 1).astype(BF)
        for j in range(LMAX + 1):
            for p in range(chips):
                parts[p][k + j] = out[p * nodes : (p + 1) * nodes, j * LANES : (j + 1) * LANES]

    by_sevens(collect)


def share_kernel(chips, *refs):
    stats, raw, refs = refs[:chips], refs[chips : 2 * chips], refs[2 * chips :]
    handed = range(2, chips, 2)
    got, refs = dict(zip(handed, refs)), refs[len(handed) :]
    weight, pack, sums_a, sums_b, share, dscore = refs[:6]
    parts, summed = refs[6 : 6 + chips], dict(zip(handed, refs[6 + chips :]))
    targets = stats[0].shape[1]
    nodes = targets // chips
    target_hit32 = hits(pack[1:2], targets, F32)
    wholes = [
        jnp.concatenate(whole_order(stats[p], chips, p, nodes), axis=1) for p in range(chips)
    ]
    top = functools.reduce(jnp.maximum, [w[0:H] for w in wholes])
    bottom = jnp.exp(-top)
    dots = jnp.zeros_like(top)
    for w in wholes:
        level = jnp.exp(w[0:H] - top)
        bottom = bottom + w[H : 2 * H] * level
        dots = dots + w[2 * H :] * level
    factors = [jnp.exp(w[0:H] - top) / bottom for w in wholes[:2]]
    at_edges = dot(
        jnp.concatenate([factors[0], dots / bottom], axis=0), target_hit32, exact=True
    )
    shares = weight[...] * at_edges[0:H]
    share[...] = shares
    sums = jnp.concatenate([sums_a[...], sums_b[...]], axis=1)
    dscore[...] = shares * (sums - at_edges[H:])
    scales = [jnp.transpose(spread(f)) for f in factors]

    def normalize(k):
        for p in range(chips):
            rows = slice(p * nodes, (p + 1) * nodes)
            here = raw[p][k].astype(F32) * scales[0][rows]
            parts[p][k] = here.astype(BF)
            if p in got:
                summed[p][k] = (here + got[p][k].astype(F32) * scales[1][rows]).astype(BF)

    each_k(normalize)


def pull_kernel(chips, second, *refs):
    some = chips // 2
    cots, refs = refs[:some], refs[some:]
    w_out, pack, table, mixed, *refs = refs
    if second:
        before, weight, own_stats, pulled, pulled0, dalpha, stats, *refs = refs
    else:
        pulled, pulled0, dalpha, *refs = refs
    incoming, total_ref = refs
    nodes = cots[0].shape[1]
    edges = pulled.shape[2]
    base = edges if second else 0
    span = some * nodes
    lines = pack[1:2, base : base + edges] - (span if second else 0)
    target_hit = hits(lines, span, BF)
    out_w = w_out[...]

    def gather(k):
        backs = [
            dot(out_w, rows_of([c[k + j] for c in cots]), 1, 1).astype(BF) for j in range(LMAX + 1)
        ]
        got = dot(rows_of(backs), target_hit).astype(BF)
        for j in range(LMAX + 1):
            incoming[k + j] = got[j * H * VH : (j + 1) * H * VH]

    by_sevens(gather)

    def emit(r, rows, lanes, total, carried):
        far = pl.ds(base + lanes.start, lanes.size)
        term = total * mixed[r, rows, far].astype(F32)
        pulled[r, rows, lanes] = total.astype(BF)
        return term if carried is None else carried + term

    def finish(rows, lanes, carried):
        total_ref[rows, lanes] = carried

    turn(table, incoming, base, range(LMAX + 1), emit, finish)
    sums = head_sum(total_ref[...])
    dalpha[...] = sums
    pulled0[...] = table[0, 0:1, base : base + edges] * incoming[0].astype(F32)
    if second:
        every = weight[...] * jnp.concatenate([before[...], sums], axis=1)
        stats[: 2 * H] = own_stats[...]
        stats[2 * H :] = dot(every, hits(pack[1:2], stats.shape[1], F32), 1, 1, exact=True)


def back_kernel(chips, *refs):
    parts, cots, firsts = refs[:chips], refs[chips : 2 * chips], refs[2 * chips : 3 * chips]
    refs = refs[3 * chips :]
    feats_own, feats_sib, pulled_a, pulled_b, pulled0_a, pulled0_b = refs[:6]
    share, dscore, query, mixed, scaled, gating, table, radial, pack, w_mix = refs[6:16]
    keep, send, dv_own, dv_sib = refs[16:20]
    dqs = refs[20 : 20 + chips]
    turned, spread_back, grads = refs[20 + chips :]
    nodes = feats_own.shape[1]
    targets = chips * nodes
    wide = H * VH
    half = grads.shape[1]

    def put(i, value):
        at = i * wide
        grads[at // half, at % half : at % half + value.shape[0]] = value

    gate = gating[...]
    zero = w_mix[0]
    shares = spread(share[...])
    dlogit = spread(dscore[...]) * (1.0 / VH**0.5)
    gates = jnp.zeros_like(gate)

    def pulled(r):
        if r == 0:
            whole = jnp.concatenate([pulled0_a[...], pulled0_b[...]], axis=1) * shares
            return (whole + dlogit * query[...]).astype(BF)
        whole = jnp.concatenate([pulled_a[r], pulled_b[r]], axis=1)
        return (whole.astype(F32) * shares).astype(BF)

    grad = jnp.zeros((wide, wide), F32)
    for r in range(LMAX + 1):
        here = scaled[r]
        down = pulled(r)
        grad = grad + dot(here, down, 1, 1)
        out = dot(zero, down)
        gates = gates + out * here.astype(F32)
        turned[r] = (out * gate).astype(BF)
    put(3, grad)
    for order in range(1, MMAX + 1):
        block = mix_block(w_mix, order, True)
        grad = jnp.zeros((2 * wide, 2 * wide), F32)
        for own, plus, minus in PAIRS:
            if own != order:
                continue
            down = rows_of([pulled(plus), pulled(minus)])
            here = rows_of([scaled[plus], scaled[minus]])
            grad = grad + dot(here, down, 1, 1)
            out = dot(block, down)
            prod = out * here.astype(F32)
            gates = gates + prod[:wide] + prod[wide:]
            turned[plus] = (out[:wide] * gate).astype(BF)
            turned[minus] = (out[wide:] * gate).astype(BF)
        put(2 + 2 * order, grad[:wide, :wide] + grad[wide:, wide:])
        put(3 + 2 * order, grad[:wide, wide:] - grad[wide:, :wide])
    dgate = (gates * (1.0 - gate)).astype(BF)
    radial_grad = dot(dgate, radial[...])
    for i in range(radial.shape[1] // wide):
        put(4 + 2 * MMAX + i, jnp.transpose(radial_grad[:, i * wide : (i + 1) * wide]))
    dq = dot(hits(pack[1:2], targets, F32), dlogit * mixed[0].astype(F32), 1, 1, exact=True)
    for p in range(chips):
        some = dq[p * nodes : (p + 1) * nodes]
        dqs[p][:nodes] = some.astype(BF)
        dqs[p][nodes:] = (some - some.astype(BF).astype(F32)).astype(BF)
    put(1, dot(rows_of([f[...] for f in firsts]), dq.astype(BF), 0, 0))

    turn_back(table, turned, range(LMAX + 1), spread_back)
    source_hit = hits(pack[0:1], 2 * nodes, BF)

    def collect(k):
        out = dot(source_hit, flat(spread_back, k), 1, 1).astype(BF)
        for j in range(LMAX + 1):
            dv_own[k + j] = out[:nodes, j * LANES : (j + 1) * LANES]
            dv_sib[k + j] = out[nodes:, j * LANES : (j + 1) * LANES]

    by_sevens(collect)
    put(0, jnp.zeros((wide, wide), F32))
    put(2, jnp.zeros((wide, wide), F32))

    def weigh(k):
        grads[0, 0:wide] += dot(flat(feats_own, k), flat(dv_own, k), 0, 0) + dot(
            flat(feats_sib, k), flat(dv_sib, k), 0, 0
        )
        total = dot(flat(parts[0], k), flat(cots[0], k), 0, 0)
        for p in range(1, chips):
            total = total + dot(flat(parts[p], k), flat(cots[p], k), 0, 0)
        grads[0, 2 * wide : 3 * wide] += total

    by_sevens(weigh)
    core = lax.axis_index("graph") % 2
    keep[...] = grads[core]
    send[...] = grads[1 - core].astype(BF)


def split_kernel(planes, keep, got, own, *outs):
    *sends, total = outs
    total[...] = (keep[...] + got[...].astype(F32)).reshape(total.shape)
    plane = lax.axis_index("dp")
    own[...] = total[plane]
    for step in range(1, planes):
        sends[step - 1][...] = total[plane ^ step].astype(BF)


def address_kernel(planes, own, *refs):
    got, refs = refs[: planes - 1], refs[planes - 1 :]
    dqs, outs = refs[: len(refs) // 2], refs[len(refs) // 2 :]
    total = functools.reduce(jnp.add, [own[...]] + [g[...].astype(F32) for g in got]).astype(BF)
    for dq, out in zip(dqs, outs):
        out[: own.shape[0]] = total
        out[own.shape[0] :] = dq[...]


def settle_kernel(*refs):
    *terms, piece, dquery = refs
    rows, nodes = piece.shape[0], dquery.shape[0]

    def total(values):
        while len(values) > 1:
            values = [a + b for a, b in zip(values[0::2], values[1::2])]
        return values[0].astype(BF)

    piece[...] = total([t[:rows].astype(F32) for t in terms])
    dquery[...] = total(
        [t[rows : rows + nodes].astype(F32) + t[rows + nodes :].astype(F32) for t in terms]
    )


def join_kernel(planes, *refs):
    mine, theirs = refs[:planes], refs[planes : 2 * planes]
    g_value, g_query, g_out, g_radial, g_mix, total = refs[2 * planes :]
    core, plane = lax.axis_index("graph") % 2, lax.axis_index("dp")
    for step in range(planes):
        total[core * planes + (plane ^ step)] = mine[step][...].astype(F32)
        total[(1 - core) * planes + (plane ^ step)] = theirs[step][...].astype(F32)
    wide = H * VH
    flat = total[...].reshape(total.shape[0] * total.shape[1], wide)
    pieces = [flat[i * wide : (i + 1) * wide] for i in range(flat.shape[0] // wide)]
    g_value[...], g_query[...], g_out[...] = pieces[:3]
    for i in range(2 * MMAX + 1):
        g_mix[i] = pieces[3 + i]
    at = 4 + 2 * MMAX
    for i in range(g_radial.shape[0] // wide):
        g_radial[i * wide : (i + 1) * wide] = pieces[at + i]


def nodes_kernel(dquery, dv_own, dv_sib, cot, w_value, w_query, out):
    value_w = w_value[...]

    def back(k):
        dv = (dv_own[k].astype(F32) + dv_sib[k].astype(F32)).astype(BF)
        return dot(dv, value_w, 1, 1)

    def one(k):
        out[k] = (cot[k].astype(F32) + back(k)).astype(BF)

    each_k(one)
    query_part = dot(dquery[...], w_query[...], 1, 1)
    out[0] = (cot[0].astype(F32) + back(0) + query_part).astype(BF)


def add_kernel(*refs):
    *terms, out = refs

    def one(k):
        out[k] = functools.reduce(jnp.add, [t[k].astype(F32) for t in terms]).astype(BF)

    each_k(one)


def update_kernel(*refs):
    *parts, feats, w_out, out = refs
    out_w = w_out[...]

    def one(k):
        total = functools.reduce(jnp.add, [t[k].astype(F32) for t in parts])
        out[k] = (feats[k].astype(F32) + dot(total.astype(BF), out_w)).astype(BF)

    each_k(one)


def call(name, us, kernel, args, outs, scratch=(), far=0, limit=24):
    whole = pl.BlockSpec(memory_space=pltpu.VMEM)
    specs = [pl.BlockSpec(memory_space=pltpu.HBM)] * far + [whole] * (len(args) - far)
    buffers = [pltpu.VMEM(s, d) for s, d in scratch]
    if far:
        buffers += [pltpu.VMEM(a.shape, a.dtype) for a in args[:far]]
        buffers += [pltpu.SemaphoreType.DMA((far,))]
    args = list(args)
    for i in range(far):
        args[i] = pltpu.with_memory_space_constraint(args[i], pltpu.HBM)
    return pl.pallas_call(
        kernel,
        out_shape=[jax.ShapeDtypeStruct(s, d) for s, d in outs],
        in_specs=specs,
        out_specs=[whole] * len(outs),
        scratch_shapes=buffers,
        compiler_params=pltpu.CompilerParams(vmem_limit_bytes=limit << 20),
        cost_estimate=pl.CostEstimate(
            flops=int(us * 1.15e9), bytes_accessed=1000, transcendentals=0
        ),
        name=name,
    )(*args)


def shards(
    node_feats,
    cotangent,
    sources,
    targets,
    bins,
    live_mask,
    radial,
    edge_bias,
    w_value,
    w_query,
    w_out,
    w_radial,
    w_mix,
    rotations,
):
    feats = jnp.transpose(node_feats[0], (1, 0, 2))
    cot = jnp.transpose(cotangent[0], (1, 0, 2))
    rot = jnp.transpose(rotations, (1, 2, 0))
    bias = jnp.transpose(edge_bias[0])
    nodes = feats.shape[1]
    wide = feats.shape[2]
    slots = sources.shape[1]
    ranks = lax.axis_size("graph")
    planes = lax.axis_size("dp")
    chips = ranks // 2
    some = chips // 2
    rank = lax.axis_index("graph")
    plane = lax.axis_index("dp")
    core, chip = rank % 2, rank // 2
    spot = chips * nodes

    def other_core(a):
        return lax.ppermute(a, "graph", [(i, i ^ 1) for i in range(ranks)])

    def along(a, step):
        return lax.ppermute(a, "graph", [(i, i ^ (2 * step)) for i in range(ranks)])

    def beside(a, step):
        return lax.ppermute(a, "dp", [(i, i ^ step) for i in range(planes)])

    def direct(a):
        return [a] + [along(a, step) for step in range(1, chips)]

    line = lax.broadcasted_iota(jnp.int32, (16, slots), 0)
    ids = jnp.where(line < 2, jnp.where(line == 0, sources, targets), jnp.where(line == 2, bins, live_mask))
    pack_own = jnp.where(
        line < 4, ids.astype(F32), jnp.pad(bias.astype(F32), ((8, 0), (0, 0)))
    )
    neighbour = along(cot, 1)
    have = {0: cot}
    step = some
    while step > 1:
        for p in list(have):
            have[p ^ step] = along(have[p], step)
        step //= 2
    pack_sib = other_core(pack_own)
    radial_sib = other_core(radial[0])
    feats_sib = other_core(feats)

    edge_f32 = ((wide, slots), F32)
    half_f32 = ((wide, slots // 2), F32)
    block = ((K, nodes, wide), BF)
    table, scaled, mixed, gating, pack, radial_here = call(
        "forward",
        9,
        functools.partial(forward_kernel, chips),
        [
            radial[0],
            w_radial,
            rot,
            feats,
            w_value,
            w_mix,
            pack_own,
            pack_sib,
            radial_sib,
            feats_sib,
        ],
        [
            ((R, 56, slots), F32),
            ((R, wide, slots), BF),
            ((R, wide, slots), BF),
            edge_f32,
            ((16, slots), F32),
            ((slots, radial.shape[2]), BF),
        ],
        [((K, wide, slots), BF)],
        far=6,
        limit=32,
    )
    first, mixed = lax.optimization_barrier((feats[0], mixed))
    firsts = direct(first)
    del have[0]
    firsts, have = lax.optimization_barrier((firsts, have))
    have[0] = cot
    have.update({p ^ 1: along(a, 1) if p else neighbour for p, a in have.items()})
    cots = [have[p] for p in range(chips)]
    weight, stats, query, *raw = call(
        "attend",
        1,
        functools.partial(attend_kernel, chips),
        [w_query, *firsts, pack, table, mixed],
        [
            ((H, slots), F32),
            ((2 * H, spot), F32),
            edge_f32,
            *([block] * chips),
        ],
        [((R, wide, slots), BF), ((K, wide, slots), BF)],
        far=1,
    )

    def pull(second, extra, sums):
        mine = slice(some, chips) if second else slice(0, some)
        return call(
            "pull",
            4 if second else 1,
            functools.partial(pull_kernel, chips, second),
            [*cots[mine], w_out, pack, table, mixed, *extra],
            [((R, wide, slots // 2), BF), half_f32, ((H, slots // 2), F32), *sums],
            [((K, wide, slots // 2), BF), half_f32],
        )

    pulled_a, pulled0_a, dalpha_a = pull(False, [], [])
    near = [along(raw[p], 1) for p in range(3, chips, 2)]
    pulled_b, pulled0_b, dalpha_b, stats = pull(
        True, [dalpha_a, weight, stats], [((3 * H, spot), F32)]
    )
    share, dscore, *parts = call(
        "share",
        0.6,
        functools.partial(share_kernel, chips),
        [*direct(stats), *raw, *near, weight, pack, dalpha_a, dalpha_b],
        [((H, slots), F32)] * 2 + [block] * (chips + len(near)),
    )
    summed = dict(zip(range(2, chips, 2), parts[chips:]))
    parts = parts[:chips]
    pending = [parts[0], along(parts[1], 1)]
    step = 2
    while step < chips:
        for p in [p for p in summed if p & step]:
            got = along(summed.pop(p), step)
            if p ^ step:
                (summed[p ^ step],) = call("add", 1, add_kernel, [summed[p ^ step], got], [block])
            else:
                pending.append(got)
        step *= 2
    total_rows = (4 + 2 * MMAX) * wide + radial.shape[2]
    cut = total_rows // (2 * planes)
    keep, send, dv_own, dv_sib, *dqs = call(
        "back",
        9,
        functools.partial(back_kernel, chips),
        [
            *parts,
            *cots,
            *firsts,
            feats,
            feats_sib,
            pulled_a,
            pulled_b,
            pulled0_a,
            pulled0_b,
            share,
            dscore,
            query,
            mixed,
            scaled,
            gating,
            table,
            radial_here,
            pack,
            w_mix,
        ],
        [
            ((total_rows // 2, wide), F32),
            ((total_rows // 2, wide), BF),
            block,
            block,
            *([((2 * nodes, wide), BF)] * chips),
        ],
        [((R, wide, slots), BF), ((K, wide, slots), BF), ((2, total_rows // 2, wide), F32)],
        limit=32,
    )
    dv_got = other_core(dv_sib)

    got = other_core(send)
    own, *sends = call(
        "split",
        0.6,
        functools.partial(split_kernel, planes),
        [keep, got],
        [((cut, wide), F32), *([((cut, wide), BF)] * (planes - 1))],
        [((planes, cut, wide), F32)],
    )
    got = [beside(sends[step - 1], step) for step in range(1, planes)]
    got, pending = lax.optimization_barrier((got, pending))
    letters = call(
        "address",
        0.6,
        functools.partial(address_kernel, planes),
        [own, *got, *dqs],
        [((cut + 2 * nodes, wide), BF)] * chips,
    )
    terms = [letters[0]] + [along(letters[step], step) for step in range(1, chips)]
    (updated,) = call("update", 2, update_kernel, [*pending, feats, w_out], [block])
    terms, updated = lax.optimization_barrier((terms, updated))
    piece, dquery = call(
        "settle", 0.6, settle_kernel, terms, [((cut, wide), BF), ((nodes, wide), BF)]
    )
    mine = [piece] + [beside(piece, step) for step in range(1, planes)]
    theirs = [other_core(a) for a in mine]
    grads = call(
        "join",
        1.5,
        functools.partial(join_kernel, planes),
        [*mine, *theirs],
        [
            ((wide, wide), F32),
            ((wide, wide), F32),
            ((wide, wide), F32),
            ((radial.shape[2], wide), F32),
            (w_mix.shape, F32),
        ],
        [((2 * planes, cut, wide), F32)],
    )

    (grad_nodes,) = call(
        "nodes",
        2.6,
        nodes_kernel,
        [dquery, dv_own, dv_got, cot, w_value, w_query],
        [block],
    )
    return (
        jnp.transpose(updated, (1, 0, 2))[None],
        jnp.transpose(grad_nodes, (1, 0, 2))[None],
        *grads,
    )


def solution(mesh):
    edge = P("dp", "graph")
    return jax.shard_map(
        shards,
        mesh=mesh,
        in_specs=(edge, edge, edge, edge, edge, edge, edge, edge, P(), P(), P(), P(), P(), P()),
        out_specs=(edge, edge, P(), P(), P(), P(), P()),
        check_vma=False,
    )
```

```python
import functools

import jax
import jax.numpy as jnp
import numpy as np
from jax import lax
from jax.experimental import pallas as pl
from jax.experimental.pallas import tpu as pltpu
from jax.sharding import PartitionSpec as P

H = 8
VH = 16
LMAX = 6
MMAX = 2
K = (LMAX + 1) ** 2
BF = jnp.bfloat16
F32 = jnp.float32
CHUNK = 16
LANES = 128


def frame_layout():
    index, degree_of = [], []
    for order in range(MMAX + 1):
        for sign in (1, -1) if order else (1,):
            for degree in range(order, LMAX + 1):
                index.append(degree * degree + degree + sign * order)
                degree_of.append(degree)
    return index, degree_of


ROWS, DEGREE = frame_layout()
R = len(ROWS)
OF_DEGREE = [[r for r in range(R) if DEGREE[r] == degree] for degree in range(LMAX + 1)]
PAIRS = []
_offset = LMAX + 1
for _order in range(1, MMAX + 1):
    _length = LMAX + 1 - _order
    for _i in range(_length):
        PAIRS.append((_order, _offset + _i, _offset + _length + _i))
    _offset += 2 * _length


def dot(a, b, ca=1, cb=0, exact=False):
    return lax.dot_general(
        a,
        b,
        (((ca,), (cb,)), ((), ())),
        precision=lax.Precision.HIGHEST if exact else None,
        preferred_element_type=F32,
    )


def flip(a):
    return jnp.transpose(a.astype(F32)).astype(a.dtype)


def hits(row, count, dtype):
    lines = lax.broadcasted_iota(jnp.int32, (count, row.shape[1]), 0)
    return jnp.where(lines == row.astype(jnp.int32), 1.0, 0.0).astype(dtype)


def head_sum(a):
    return jnp.sum(a.reshape(H, VH, a.shape[1]), axis=1)


def spread(a):
    return jnp.broadcast_to(a[:, None, :], (H, VH, a.shape[1])).reshape(H * VH, a.shape[1])


def turn(table, source, base, degrees, emit, finish=None):
    channels, edges = source.shape[1], source.shape[2]

    def step(i, carry):
        rows = pl.ds(i * CHUNK, CHUNK)
        for start in range(0, edges, LANES):
            lanes = pl.ds(start, LANES)
            carried = None
            for degree in degrees:
                block = range(degree * degree, (degree + 1) ** 2)
                parts = [source[k, rows, lanes].astype(F32) for k in block]
                for r in OF_DEGREE[degree]:
                    total = None
                    for k, part in zip(block, parts):
                        at = base + start
                        term = table[r, k : k + 1, at : at + LANES] * part
                        total = term if total is None else total + term
                    carried = emit(r, rows, lanes, total, carried)
            if finish is not None:
                finish(rows, lanes, carried)
        return carry

    for i in range(channels // CHUNK):
        step(i, 0)


def turn_back(table, source, degrees, out):
    channels, edges = source.shape[1], source.shape[2]

    def step(i, carry):
        rows = pl.ds(i * CHUNK, CHUNK)
        for start in range(0, edges, LANES):
            lanes = pl.ds(start, LANES)
            for degree in degrees:
                parts = [source[r, rows, lanes].astype(F32) for r in OF_DEGREE[degree]]
                for k in range(degree * degree, (degree + 1) ** 2):
                    total = None
                    for r, part in zip(OF_DEGREE[degree], parts):
                        term = table[r, k : k + 1, start : start + LANES] * part
                        total = term if total is None else total + term
                    out[k, rows, lanes] = total.astype(out.dtype)
        return carry

    for i in range(channels // CHUNK):
        step(i, 0)


def by_sevens(body):
    for i in range(LMAX + 1):
        body(i * (LMAX + 1))


def each_k(body):
    by_sevens(lambda k: [body(k + j) for j in range(LMAX + 1)] and None)


def flat(ref, k):
    return ref[pl.ds(k, LMAX + 1)].reshape((LMAX + 1) * ref.shape[1], ref.shape[2])


def rows_of(pieces):
    return jnp.concatenate(pieces, axis=0)


def whole_order(own, chips, p, span):
    return [own[:, (q ^ p) * span : ((q ^ p) + 1) * span] for q in range(chips)]


def mix_block(w_mix, order, back):
    even, odd = w_mix[2 * order - 1], w_mix[2 * order]
    if back:
        return jnp.concatenate(
            [
                jnp.concatenate([even, odd], axis=1),
                jnp.concatenate([-odd, even], axis=1),
            ],
            axis=0,
        )
    even, odd = flip(even), flip(odd)
    return jnp.concatenate(
        [
            jnp.concatenate([even, -odd], axis=1),
            jnp.concatenate([odd, even], axis=1),
        ],
        axis=0,
    )


def forward_kernel(chips, *refs):
    far, refs = refs[:6], refs[6:]
    pack_own, pack_sib, radial_sib, feats_sib, *refs = refs
    table, scaled, mixed, gating, pack, radial, incoming, *refs = refs
    near, sems = refs[:6], refs[6]
    copies = [pltpu.make_async_copy(a, b, sems.at[i]) for i, (a, b) in enumerate(zip(far, near))]
    for c in copies:
        c.start()
    radial_own, w_radial, rot, feats_own, w_value, w_mix = near
    rank = lax.axis_index("graph")
    core, chip = rank % 2, rank // 2
    slots = pack_own.shape[1]
    cap = slots // (2 * chips)
    nodes = feats_sib.shape[1]
    bins = rot.shape[2]

    edge = lax.broadcasted_iota(jnp.int32, (1, slots), 1)
    place = lax.broadcasted_iota(jnp.int32, (2 * slots, slots), 0)
    side = (edge // cap) % 2
    origin = side * slots + (2 * ((edge // (2 * cap)) ^ chip) + core) * cap + edge % cap
    pick = jnp.where(place == origin, 1.0, 0.0).astype(BF)

    def relative(raw):
        ids = raw[0:2].astype(jnp.int32)
        owner = ids[1:2] // nodes
        source = ids[0:1] - 2 * chip * nodes
        swapped = jnp.where(source < nodes, source + nodes, source - nodes)
        rows_ = [jnp.where(core == 0, source, swapped), ids[1:2] - owner * nodes]
        rows_ = [a.astype(F32) for a in rows_ + [(owner // 2) ^ chip]]
        return jnp.concatenate([rows_[0], rows_[1], raw[2:4], rows_[2], raw[5:]], axis=0)

    packs = [relative(pack_own[...]), relative(pack_sib[...])]
    packs = jnp.concatenate(packs, axis=1).astype(BF)
    rows = dot(packs, pick)
    lines = rows[4:5] * float(nodes) + rows[1:2]
    pack[...] = rows
    pack[1:2, :] = lines
    bin_hit = hits(rows[2:3], bins, BF)
    source_hit = hits(rows[0:1], 2 * nodes, BF)
    for c in copies[:2]:
        c.wait()
    radial[...] = dot(pick, rows_of([radial_own[...], radial_sib[...]]), 0, 0).astype(BF)
    gating[...] = jax.nn.sigmoid(dot(flip(w_radial[...]), radial[...], 1, 1))
    copies[2].wait()
    for r, row in enumerate(ROWS):
        table[r, 0:K, :] = dot(rot[row], bin_hit)
    for c in copies[3:]:
        c.wait()
    value_t = flip(w_value[...])

    def gather(k):
        values = [
            dot(value_t, rows_of([feats_own[k + j], feats_sib[k + j]]), 1, 1).astype(BF)
            for j in range(LMAX + 1)
        ]
        got = dot(rows_of(values), source_hit).astype(BF)
        for j in range(LMAX + 1):
            incoming[k + j] = got[j * H * VH : (j + 1) * H * VH]

    by_sevens(gather)

    def emit(r, rows_, lanes, total, carried):
        gate = gating[rows_, lanes] if carried is None else carried
        scaled[r, rows_, lanes] = (total * gate).astype(BF)
        return gate

    turn(table, incoming, 0, range(LMAX + 1), emit)

    zero_t = flip(w_mix[0])
    for r in range(LMAX + 1):
        mixed[r] = dot(zero_t, scaled[r]).astype(BF)
    blocks = [None] + [mix_block(w_mix, order, False) for order in range(1, MMAX + 1)]
    for order, plus, minus in PAIRS:
        out = dot(blocks[order], rows_of([scaled[plus], scaled[minus]])).astype(BF)
        mixed[plus] = out[: H * VH]
        mixed[minus] = out[H * VH :]


def attend_kernel(chips, *refs):
    far, refs = refs[0], refs[1:]
    firsts, refs = refs[:chips], refs[chips:]
    pack, table, mixed, weight, stats, query, *refs = refs
    parts, refs = refs[:chips], refs[chips:]
    scaled_rows, back, w_query, sems = refs
    copy = pltpu.make_async_copy(far, w_query, sems.at[0])
    copy.start()
    slots = pack.shape[1]
    nodes = firsts[0].shape[0]
    targets = chips * nodes
    rows = pack[...]
    target_hit = hits(rows[1:2], targets, BF)
    first = rows_of([f[...] for f in firsts])
    copy.wait()
    queries = dot(flip(w_query[...]), first, 1, 1).astype(BF)
    query[...] = dot(queries, target_hit)
    scores = head_sum(mixed[0].astype(F32) * query[...]) * (1.0 / VH**0.5) + rows[8:16]
    live = rows[3:4] > 0.5
    columns = jnp.transpose(rows)
    score_columns = jnp.transpose(scores)
    line = lax.broadcasted_iota(jnp.int32, (slots, targets), 1)
    chosen = (line == columns[:, 1:2].astype(jnp.int32)) & (columns[:, 3:4] > 0.5)
    top = jnp.concatenate(
        [
            jnp.max(jnp.where(chosen, score_columns[:, h : h + 1], 0.0), axis=0, keepdims=True)
            for h in range(H)
        ],
        axis=0,
    )
    top = jnp.maximum(top, 0.0)
    target_hit32 = target_hit.astype(F32)
    top_edge = dot(top, target_hit32, exact=True)
    weights = jnp.where(live, jnp.exp(jnp.where(live, scores - top_edge, 0.0)), 0.0)
    weight[...] = weights
    stats[0:H] = top
    stats[H : 2 * H] = dot(weights, target_hit32, 1, 1, exact=True)

    wide = spread(weights)
    for r in range(R):
        scaled_rows[r] = (mixed[r].astype(F32) * wide).astype(BF)
    turn_back(table, scaled_rows, range(LMAX + 1), back)

    def collect(k):
        out = dot(target_hit, flat(back, k), 1, 1).astype(BF)
        for j in range(LMAX + 1):
            for p in range(chips):
                parts[p][k + j] = out[p * nodes : (p + 1) * nodes, j * LANES : (j + 1) * LANES]

    by_sevens(collect)


def share_kernel(chips, *refs):
    stats, raw, refs = refs[:chips], refs[chips : 2 * chips], refs[2 * chips :]
    handed = range(2, chips, 2)
    got, refs = dict(zip(handed, refs)), refs[len(handed) :]
    weight, pack, sums_a, sums_b, share, dscore = refs[:6]
    parts, summed = refs[6 : 6 + chips], dict(zip(handed, refs[6 + chips :]))
    targets = stats[0].shape[1]
    nodes = targets // chips
    target_hit32 = hits(pack[1:2], targets, F32)
    wholes = [
        jnp.concatenate(whole_order(stats[p], chips, p, nodes), axis=1) for p in range(chips)
    ]
    top = functools.reduce(jnp.maximum, [w[0:H] for w in wholes])
    bottom = jnp.exp(-top)
    dots = jnp.zeros_like(top)
    for w in wholes:
        level = jnp.exp(w[0:H] - top)
        bottom = bottom + w[H : 2 * H] * level
        dots = dots + w[2 * H :] * level
    factors = [jnp.exp(w[0:H] - top) / bottom for w in wholes[:2]]
    at_edges = dot(
        jnp.concatenate([factors[0], dots / bottom], axis=0), target_hit32, exact=True
    )
    shares = weight[...] * at_edges[0:H]
    share[...] = shares
    sums = jnp.concatenate([sums_a[...], sums_b[...]], axis=1)
    dscore[...] = shares * (sums - at_edges[H:])
    scales = [jnp.transpose(spread(f)) for f in factors]

    def normalize(k):
        for p in range(chips):
            rows = slice(p * nodes, (p + 1) * nodes)
            here = raw[p][k].astype(F32) * scales[0][rows]
            parts[p][k] = here.astype(BF)
            if p in got:
                summed[p][k] = (here + got[p][k].astype(F32) * scales[1][rows]).astype(BF)

    each_k(normalize)


def pull_kernel(chips, second, *refs):
    some = chips // 2
    cots, refs = refs[:some], refs[some:]
    w_out, pack, table, mixed, *refs = refs
    if second:
        before, weight, own_stats, pulled, pulled0, dalpha, stats, *refs = refs
    else:
        pulled, pulled0, dalpha, *refs = refs
    incoming, total_ref = refs
    nodes = cots[0].shape[1]
    edges = pulled.shape[2]
    base = edges if second else 0
    span = some * nodes
    lines = pack[1:2, base : base + edges] - (span if second else 0)
    target_hit = hits(lines, span, BF)
    out_w = w_out[...]

    def gather(k):
        backs = [
            dot(out_w, rows_of([c[k + j] for c in cots]), 1, 1).astype(BF) for j in range(LMAX + 1)
        ]
        got = dot(rows_of(backs), target_hit).astype(BF)
        for j in range(LMAX + 1):
            incoming[k + j] = got[j * H * VH : (j + 1) * H * VH]

    by_sevens(gather)

    def emit(r, rows, lanes, total, carried):
        far = pl.ds(base + lanes.start, lanes.size)
        term = total * mixed[r, rows, far].astype(F32)
        pulled[r, rows, lanes] = total.astype(BF)
        return term if carried is None else carried + term

    def finish(rows, lanes, carried):
        total_ref[rows, lanes] = carried

    turn(table, incoming, base, range(LMAX + 1), emit, finish)
    sums = head_sum(total_ref[...])
    dalpha[...] = sums
    pulled0[...] = table[0, 0:1, base : base + edges] * incoming[0].astype(F32)
    if second:
        every = weight[...] * jnp.concatenate([before[...], sums], axis=1)
        stats[: 2 * H] = own_stats[...]
        stats[2 * H :] = dot(every, hits(pack[1:2], stats.shape[1], F32), 1, 1, exact=True)


def back_kernel(chips, *refs):
    parts, cots, firsts = refs[:chips], refs[chips : 2 * chips], refs[2 * chips : 3 * chips]
    refs = refs[3 * chips :]
    feats_own, feats_sib, pulled_a, pulled_b, pulled0_a, pulled0_b = refs[:6]
    share, dscore, query, mixed, scaled, gating, table, radial, pack, w_mix = refs[6:16]
    keep, send, dv_own, dv_sib = refs[16:20]
    dqs = refs[20 : 20 + chips]
    turned, spread_back, grads = refs[20 + chips :]
    nodes = feats_own.shape[1]
    targets = chips * nodes
    wide = H * VH
    half = grads.shape[1]

    def put(i, value):
        at = i * wide
        grads[at // half, at % half : at % half + value.shape[0]] = value

    gate = gating[...]
    zero = w_mix[0]
    shares = spread(share[...])
    dlogit = spread(dscore[...]) * (1.0 / VH**0.5)
    gates = jnp.zeros_like(gate)

    def pulled(r):
        if r == 0:
            whole = jnp.concatenate([pulled0_a[...], pulled0_b[...]], axis=1) * shares
            return (whole + dlogit * query[...]).astype(BF)
        whole = jnp.concatenate([pulled_a[r], pulled_b[r]], axis=1)
        return (whole.astype(F32) * shares).astype(BF)

    grad = jnp.zeros((wide, wide), F32)
    for r in range(LMAX + 1):
        here = scaled[r]
        down = pulled(r)
        grad = grad + dot(here, down, 1, 1)
        out = dot(zero, down)
        gates = gates + out * here.astype(F32)
        turned[r] = (out * gate).astype(BF)
    put(3, grad)
    for order in range(1, MMAX + 1):
        block = mix_block(w_mix, order, True)
        grad = jnp.zeros((2 * wide, 2 * wide), F32)
        for own, plus, minus in PAIRS:
            if own != order:
                continue
            down = rows_of([pulled(plus), pulled(minus)])
            here = rows_of([scaled[plus], scaled[minus]])
            grad = grad + dot(here, down, 1, 1)
            out = dot(block, down)
            prod = out * here.astype(F32)
            gates = gates + prod[:wide] + prod[wide:]
            turned[plus] = (out[:wide] * gate).astype(BF)
            turned[minus] = (out[wide:] * gate).astype(BF)
        put(2 + 2 * order, grad[:wide, :wide] + grad[wide:, wide:])
        put(3 + 2 * order, grad[:wide, wide:] - grad[wide:, :wide])
    dgate = (gates * (1.0 - gate)).astype(BF)
    radial_grad = dot(dgate, radial[...])
    for i in range(radial.shape[1] // wide):
        put(4 + 2 * MMAX + i, jnp.transpose(radial_grad[:, i * wide : (i + 1) * wide]))
    dq = dot(hits(pack[1:2], targets, F32), dlogit * mixed[0].astype(F32), 1, 1, exact=True)
    for p in range(chips):
        some = dq[p * nodes : (p + 1) * nodes]
        dqs[p][:nodes] = some.astype(BF)
        dqs[p][nodes:] = (some - some.astype(BF).astype(F32)).astype(BF)
    put(1, dot(rows_of([f[...] for f in firsts]), dq.astype(BF), 0, 0))

    turn_back(table, turned, range(LMAX + 1), spread_back)
    source_hit = hits(pack[0:1], 2 * nodes, BF)

    def collect(k):
        out = dot(source_hit, flat(spread_back, k), 1, 1).astype(BF)
        for j in range(LMAX + 1):
            dv_own[k + j] = out[:nodes, j * LANES : (j + 1) * LANES]
            dv_sib[k + j] = out[nodes:, j * LANES : (j + 1) * LANES]

    by_sevens(collect)
    put(0, jnp.zeros((wide, wide), F32))
    put(2, jnp.zeros((wide, wide), F32))

    def weigh(k):
        grads[0, 0:wide] += dot(flat(feats_own, k), flat(dv_own, k), 0, 0) + dot(
            flat(feats_sib, k), flat(dv_sib, k), 0, 0
        )
        total = dot(flat(parts[0], k), flat(cots[0], k), 0, 0)
        for p in range(1, chips):
            total = total + dot(flat(parts[p], k), flat(cots[p], k), 0, 0)
        grads[0, 2 * wide : 3 * wide] += total

    by_sevens(weigh)
    core = lax.axis_index("graph") % 2
    keep[...] = grads[core]
    send[...] = grads[1 - core].astype(BF)


def split_kernel(planes, keep, got, own, *outs):
    *sends, total = outs
    total[...] = (keep[...] + got[...].astype(F32)).reshape(total.shape)
    plane = lax.axis_index("dp")
    own[...] = total[plane]
    for step in range(1, planes):
        sends[step - 1][...] = total[plane ^ step].astype(BF)


def address_kernel(planes, own, *refs):
    got, refs = refs[: planes - 1], refs[planes - 1 :]
    dqs, outs = refs[: len(refs) // 2], refs[len(refs) // 2 :]
    total = functools.reduce(jnp.add, [own[...]] + [g[...].astype(F32) for g in got]).astype(BF)
    for dq, out in zip(dqs, outs):
        out[: own.shape[0]] = total
        out[own.shape[0] :] = dq[...]


def settle_kernel(*refs):
    *terms, piece, dquery = refs
    rows, nodes = piece.shape[0], dquery.shape[0]

    def total(values):
        while len(values) > 1:
            values = [a + b for a, b in zip(values[0::2], values[1::2])]
        return values[0].astype(BF)

    piece[...] = total([t[:rows].astype(F32) for t in terms])
    dquery[...] = total(
        [t[rows : rows + nodes].astype(F32) + t[rows + nodes :].astype(F32) for t in terms]
    )


def join_kernel(planes, *refs):
    mine, theirs = refs[:planes], refs[planes : 2 * planes]
    g_value, g_query, g_out, g_radial, g_mix, total = refs[2 * planes :]
    core, plane = lax.axis_index("graph") % 2, lax.axis_index("dp")
    for step in range(planes):
        total[core * planes + (plane ^ step)] = mine[step][...].astype(F32)
        total[(1 - core) * planes + (plane ^ step)] = theirs[step][...].astype(F32)
    wide = H * VH
    flat = total[...].reshape(total.shape[0] * total.shape[1], wide)
    pieces = [flat[i * wide : (i + 1) * wide] for i in range(flat.shape[0] // wide)]
    g_value[...], g_query[...], g_out[...] = pieces[:3]
    for i in range(2 * MMAX + 1):
        g_mix[i] = pieces[3 + i]
    at = 4 + 2 * MMAX
    for i in range(g_radial.shape[0] // wide):
        g_radial[i * wide : (i + 1) * wide] = pieces[at + i]


def nodes_kernel(dquery, dv_own, dv_sib, cot, w_value, w_query, out):
    value_w = w_value[...]

    def back(k):
        dv = (dv_own[k].astype(F32) + dv_sib[k].astype(F32)).astype(BF)
        return dot(dv, value_w, 1, 1)

    def one(k):
        out[k] = (cot[k].astype(F32) + back(k)).astype(BF)

    each_k(one)
    query_part = dot(dquery[...], w_query[...], 1, 1)
    out[0] = (cot[0].astype(F32) + back(0) + query_part).astype(BF)


def add_kernel(*refs):
    *terms, out = refs

    def one(k):
        out[k] = functools.reduce(jnp.add, [t[k].astype(F32) for t in terms]).astype(BF)

    each_k(one)


def update_kernel(*refs):
    *parts, feats, w_out, out = refs
    out_w = w_out[...]

    def one(k):
        total = functools.reduce(jnp.add, [t[k].astype(F32) for t in parts])
        out[k] = (feats[k].astype(F32) + dot(total.astype(BF), out_w)).astype(BF)

    each_k(one)


def call(name, us, kernel, args, outs, scratch=(), far=0, limit=24):
    whole = pl.BlockSpec(memory_space=pltpu.VMEM)
    specs = [pl.BlockSpec(memory_space=pltpu.HBM)] * far + [whole] * (len(args) - far)
    buffers = [pltpu.VMEM(s, d) for s, d in scratch]
    if far:
        buffers += [pltpu.VMEM(a.shape, a.dtype) for a in args[:far]]
        buffers += [pltpu.SemaphoreType.DMA((far,))]
    args = list(args)
    for i in range(far):
        args[i] = pltpu.with_memory_space_constraint(args[i], pltpu.HBM)
    return pl.pallas_call(
        kernel,
        out_shape=[jax.ShapeDtypeStruct(s, d) for s, d in outs],
        in_specs=specs,
        out_specs=[whole] * len(outs),
        scratch_shapes=buffers,
        compiler_params=pltpu.CompilerParams(vmem_limit_bytes=limit << 20),
        cost_estimate=pl.CostEstimate(
            flops=int(us * 1.15e9), bytes_accessed=1000, transcendentals=0
        ),
        name=name,
    )(*args)


def shards(
    node_feats,
    cotangent,
    sources,
    targets,
    bins,
    live_mask,
    radial,
    edge_bias,
    w_value,
    w_query,
    w_out,
    w_radial,
    w_mix,
    rotations,
):
    feats = jnp.transpose(node_feats[0], (1, 0, 2))
    cot = jnp.transpose(cotangent[0], (1, 0, 2))
    rot = jnp.transpose(rotations, (1, 2, 0))
    bias = jnp.transpose(edge_bias[0])
    nodes = feats.shape[1]
    wide = feats.shape[2]
    slots = sources.shape[1]
    ranks = lax.axis_size("graph")
    planes = lax.axis_size("dp")
    chips = ranks // 2
    some = chips // 2
    rank = lax.axis_index("graph")
    plane = lax.axis_index("dp")
    core, chip = rank % 2, rank // 2
    spot = chips * nodes

    def other_core(a):
        return lax.ppermute(a, "graph", [(i, i ^ 1) for i in range(ranks)])

    def along(a, step):
        return lax.ppermute(a, "graph", [(i, i ^ (2 * step)) for i in range(ranks)])

    def beside(a, step):
        return lax.ppermute(a, "dp", [(i, i ^ step) for i in range(planes)])

    def direct(a):
        return [a] + [along(a, step) for step in range(1, chips)]

    line = lax.broadcasted_iota(jnp.int32, (16, slots), 0)
    ids = jnp.where(line < 2, jnp.where(line == 0, sources, targets), jnp.where(line == 2, bins, live_mask))
    pack_own = jnp.where(
        line < 4, ids.astype(F32), jnp.pad(bias.astype(F32), ((8, 0), (0, 0)))
    )
    neighbour = along(cot, 1)
    have = {0: cot}
    step = some
    while step > 1:
        for p in list(have):
            have[p ^ step] = along(have[p], step)
        step //= 2
    pack_sib = other_core(pack_own)
    radial_sib = other_core(radial[0])
    feats_sib = other_core(feats)

    edge_f32 = ((wide, slots), F32)
    half_f32 = ((wide, slots // 2), F32)
    block = ((K, nodes, wide), BF)
    table, scaled, mixed, gating, pack, radial_here = call(
        "forward",
        9,
        functools.partial(forward_kernel, chips),
        [
            radial[0],
            w_radial,
            rot,
            feats,
            w_value,
            w_mix,
            pack_own,
            pack_sib,
            radial_sib,
            feats_sib,
        ],
        [
            ((R, 56, slots), F32),
            ((R, wide, slots), BF),
            ((R, wide, slots), BF),
            edge_f32,
            ((16, slots), F32),
            ((slots, radial.shape[2]), BF),
        ],
        [((K, wide, slots), BF)],
        far=6,
        limit=32,
    )
    first, mixed = lax.optimization_barrier((feats[0], mixed))
    firsts = direct(first)
    del have[0]
    firsts, have = lax.optimization_barrier((firsts, have))
    have[0] = cot
    have.update({p ^ 1: along(a, 1) if p else neighbour for p, a in have.items()})
    cots = [have[p] for p in range(chips)]
    weight, stats, query, *raw = call(
        "attend",
        1,
        functools.partial(attend_kernel, chips),
        [w_query, *firsts, pack, table, mixed],
        [
            ((H, slots), F32),
            ((2 * H, spot), F32),
            edge_f32,
            *([block] * chips),
        ],
        [((R, wide, slots), BF), ((K, wide, slots), BF)],
        far=1,
    )

    def pull(second, extra, sums):
        mine = slice(some, chips) if second else slice(0, some)
        return call(
            "pull",
            4 if second else 1,
            functools.partial(pull_kernel, chips, second),
            [*cots[mine], w_out, pack, table, mixed, *extra],
            [((R, wide, slots // 2), BF), half_f32, ((H, slots // 2), F32), *sums],
            [((K, wide, slots // 2), BF), half_f32],
        )

    pulled_a, pulled0_a, dalpha_a = pull(False, [], [])
    near = [along(raw[p], 1) for p in range(3, chips, 2)]
    pulled_b, pulled0_b, dalpha_b, stats = pull(
        True, [dalpha_a, weight, stats], [((3 * H, spot), F32)]
    )
    share, dscore, *parts = call(
        "share",
        0.6,
        functools.partial(share_kernel, chips),
        [*direct(stats), *raw, *near, weight, pack, dalpha_a, dalpha_b],
        [((H, slots), F32)] * 2 + [block] * (chips + len(near)),
    )
    summed = dict(zip(range(2, chips, 2), parts[chips:]))
    parts = parts[:chips]
    pending = [parts[0], along(parts[1], 1)]
    step = 2
    while step < chips:
        for p in [p for p in summed if p & step]:
            got = along(summed.pop(p), step)
            if p ^ step:
                (summed[p ^ step],) = call("add", 1, add_kernel, [summed[p ^ step], got], [block])
            else:
                pending.append(got)
        step *= 2
    total_rows = (4 + 2 * MMAX) * wide + radial.shape[2]
    cut = total_rows // (2 * planes)
    keep, send, dv_own, dv_sib, *dqs = call(
        "back",
        9,
        functools.partial(back_kernel, chips),
        [
            *parts,
            *cots,
            *firsts,
            feats,
            feats_sib,
            pulled_a,
            pulled_b,
            pulled0_a,
            pulled0_b,
            share,
            dscore,
            query,
            mixed,
            scaled,
            gating,
            table,
            radial_here,
            pack,
            w_mix,
        ],
        [
            ((total_rows // 2, wide), F32),
            ((total_rows // 2, wide), BF),
            block,
            block,
            *([((2 * nodes, wide), BF)] * chips),
        ],
        [((R, wide, slots), BF), ((K, wide, slots), BF), ((2, total_rows // 2, wide), F32)],
        limit=32,
    )
    dv_got = other_core(dv_sib)

    got = other_core(send)
    own, *sends = call(
        "split",
        0.6,
        functools.partial(split_kernel, planes),
        [keep, got],
        [((cut, wide), F32), *([((cut, wide), BF)] * (planes - 1))],
        [((planes, cut, wide), F32)],
    )
    got = [beside(sends[step - 1], step) for step in reversed(range(1, planes))]
    letters = call(
        "address",
        0.6,
        functools.partial(address_kernel, planes),
        [own, *got, *dqs],
        [((cut + 2 * nodes, wide), BF)] * chips,
    )
    terms = [letters[0]] + [along(letters[step], step) for step in range(1, chips)]
    (updated,) = call("update", 2, update_kernel, [*pending, feats, w_out], [block])
    terms, updated = lax.optimization_barrier((terms, updated))
    piece, dquery = call(
        "settle", 0.6, settle_kernel, terms, [((cut, wide), BF), ((nodes, wide), BF)]
    )
    mine = [piece] + [beside(piece, step) for step in range(1, planes)]
    theirs = [other_core(a) for a in mine]
    grads = call(
        "join",
        1.5,
        functools.partial(join_kernel, planes),
        [*mine, *theirs],
        [
            ((wide, wide), F32),
            ((wide, wide), F32),
            ((wide, wide), F32),
            ((radial.shape[2], wide), F32),
            (w_mix.shape, F32),
        ],
        [((2 * planes, cut, wide), F32)],
    )

    (grad_nodes,) = call(
        "nodes",
        2.6,
        nodes_kernel,
        [dquery, dv_own, dv_got, cot, w_value, w_query],
        [block],
    )
    return (
        jnp.transpose(updated, (1, 0, 2))[None],
        jnp.transpose(grad_nodes, (1, 0, 2))[None],
        *grads,
    )


def solution(mesh):
    edge = P("dp", "graph")
    return jax.shard_map(
        shards,
        mesh=mesh,
        in_specs=(edge, edge, edge, edge, edge, edge, edge, edge, P(), P(), P(), P(), P(), P()),
        out_specs=(edge, edge, P(), P(), P(), P(), P()),
        check_vma=False,
    )
```
